256 devices in a mesh: tm: 8 (over x, y_hi), rows: 32 (over z, y_lo, core).
Axes of the slice: x: 4, y: 4 (y_hi: 2, y_lo: 2; y = y_hi * 2 + y_lo), z: 8, core: 2. Of those that a mesh axis runs over, the one named last changes fastest.
Arguments:
- start_state: float32 [2, 1024, 4096], P(None, 'rows'), may hold values from -6 to 6
- guess: float32 [8, 2, 1024, 4096], P('tm', None, 'rows'), may hold values from -6 to 6
Outputs:
- corrected: float32 [8, 2, 1024, 4096], P('tm', None, 'rows')
- relaxed: float32 [8, 2, 1024, 4096], P('tm', None, 'rows')
The draws below stay inside these ranges and needn't reach their ends.
All inputs are finite; a program needn't handle non-finite values.
Results may differ from the reference program's by a relative error of at most 0.00002.
Values sent between devices are 32-bit elements; how exact they have to be, the bound alone decides.
A program may use at most 64 MiB of HBM per device.

```python
import jax
import jax.numpy as jnp
from jax import lax

NCOLS = 4096
STEPS = 4
GROUPS = 8
NROWS = 1024


def shard_levels(stream_key, extent, shards, low, largest):
    loudness, own = 1.0, jax.random.fold_in(stream_key, 6)
    for dim, parts in shards:
        steps = jnp.exp(jax.random.uniform(jax.random.fold_in(own, dim), (parts,), jnp.float32, low / len(shards), largest / len(shards)))
        loudness = loudness * jnp.repeat(steps, extent[dim] // parts).reshape([-1 if axis == dim else 1 for axis in range(len(extent))])
    return loudness


def noise(own_key, extent, width, limit, cuts=(), dtype=jnp.bfloat16):
    result = width * jax.random.normal(own_key, extent, jnp.float32)
    if cuts:
        result = result * shard_levels(own_key, extent, cuts, -0.22, 0.18)
    return jnp.clip(result, -limit, limit).astype(dtype)


def setup_inputs(seed: int = 0) -> dict:
    key_list = jax.random.split(jax.random.key(seed), 3)
    start_state = noise(key_list[0], (2, NROWS, NCOLS), 1.0, 6.0, ((1, 32),), jnp.float32)
    guess = noise(key_list[1], (GROUPS, 2, NROWS, NCOLS), 0.8, 6.0, ((0, 8), (2, 32)), jnp.float32)
    return dict(start_state=start_state, guess=guess)


fine_dt = 0.05
viscosity = 1.0


def advance_whole(field, size):
    east = jnp.roll(field, -1, 2)
    west = jnp.roll(field, 1, 2)
    upper = jnp.roll(field, -1, 1)
    lower = jnp.roll(field, 1, 1)
    grad_x = 0.5 * (east - west)
    grad_y = 0.5 * (upper - lower)
    lap = east + west + upper + lower - 4.0 * field
    return field + size * (viscosity * lap - field[0:1] * grad_x - field[1:2] * grad_y)


def fine_march(field):
    for step in range(STEPS):
        field = advance_whole(field, fine_dt)
    return field


def coarse_march(field):
    return advance_whole(field, STEPS * fine_dt)


def reference(start_state, guess):
    prior = jnp.concatenate([start_state[None], guess[:-1]], axis=0)
    relaxed = lax.map(fine_march, prior)
    again = jnp.concatenate([start_state[None], relaxed[:-1]], axis=0)
    tau = lax.map(lambda f: fine_march(f) - coarse_march(f), again)

    def recurse(carry, term):
        nxt = coarse_march(carry) + term
        return nxt, nxt

    final, corrected = lax.scan(recurse, start_state, tau)
    return corrected, relaxed
```

```python
import functools

import jax
import jax.numpy as jnp
from jax import lax
from jax.experimental import pallas as pl
from jax.experimental.pallas import tpu as pltpu
from jax.sharding import PartitionSpec as P

STEPS = 4
FINE = 0.05
COARSE = STEPS * FINE
VISCOSITY = 1.0
MESH = pl.DeviceIdType.MESH

LANES = 128
TOP = 16
FRAME = 64
HALO = 10
EDGE = 2
WIDE = 8
SPAN = WIDE + 2
GROUP = 2


def update(src, base, i, count, row, rows, size):
    lane = lax.broadcasted_iota(jnp.int32, (2, rows, LANES), 2)
    here = pl.ds(row, rows)
    left = base + jnp.maximum(i - 1, 0)
    right = base + jnp.minimum(i + 1, count - 1)
    c = src[base + i, :, here, :]
    east = pltpu.roll(jnp.where(lane == 0, src[right, :, here, :], c), LANES - 1, 2)
    west = pltpu.roll(jnp.where(lane == LANES - 1, src[left, :, here, :], c), 1, 2)
    upper = src[base + i, :, pl.ds(row + 1, rows), :]
    lower = src[base + i, :, pl.ds(row - 1, rows), :]
    u = (0.5 * size) * c[0:1]
    v = (0.5 * size) * c[1:2]
    k = size * VISCOSITY
    return (1.0 - 4.0 * k) * c + ((k - u) * east + (k + u) * west) + ((k - v) * upper + (k + v) * lower)


def kernel(
    cols, groups, strips, start_ref, guess_ref, corrected_ref, relaxed_ref,
    field, tau, w0, w1, w2, relaxed, state, mid, nxt,
    load_sem, arrive_sem, shift_sem, halo_send, halo_recv, chain_send, chain_recv, out_sem,
):
    g = lax.axis_index("tm")
    r = lax.axis_index("rows")
    x = g // 2
    up = lax.rem(r + 1, strips)
    down = lax.rem(r + strips - 1, strips)
    n_windows = cols // WIDE
    n_groups = cols // GROUP
    strip = pl.ds(TOP, 32)
    S, B, A = 0, 1, 2

    barrier = pltpu.get_barrier_semaphore()

    def greet(group, row):
        pl.semaphore_signal(barrier, inc=1, device_id=(group, row), device_id_type=MESH)

    greet(g, up)
    greet(g, down)

    @pl.when(g >= 1)
    def _():
        greet(g - 1, r)

    @pl.when(g >= 2)
    def _():
        greet(g - 2, r)
        greet(g - 2, up)
        greet(g - 2, down)

    def load(src, which, sem):
        def one(f, _):
            c = lax.rem(f + cols - 1, cols)
            pltpu.make_async_copy(
                src.at[:, :, pl.ds(pl.multiple_of(c * LANES, LANES), LANES)],
                field.at[which, f, :, strip, :],
                sem(f),
            ).start()
            return 0

        lax.fori_loop(0, cols, one, 0)

    def chunk(k):
        if k == 0:
            return 0, SPAN
        if k < n_windows - 1:
            return WIDE * k + 2, WIDE
        return WIDE * k + 2, WIDE - 2

    load(guess_ref, B, lambda f: load_sem.at[0])

    @pl.when(g == 0)
    def _():
        for k in range(n_windows):
            lo, n = chunk(k)

            def one(f, _, k=k):
                c = lax.rem(f + cols - 1, cols)
                pltpu.make_async_copy(
                    start_ref.at[:, :, pl.ds(pl.multiple_of(c * LANES, LANES), LANES)],
                    field.at[A, f, :, strip, :],
                    arrive_sem.at[k],
                ).start()
                return 0

            lax.fori_loop(lo, lo + n, one, 0)

    @pl.when(g == 1)
    def _():
        load(start_ref, S, lambda f: load_sem.at[1])

    pl.semaphore_wait(barrier, 2 + jnp.where(g < groups - 1, 1, 0) + jnp.where(g < groups - 2, 3, 0))

    def whole(which, lo, n):
        return field.at[which, pl.ds(lo, n), :, strip, :]

    def shift(k):
        lo, n = chunk(k)
        return pltpu.make_async_remote_copy(
            src_ref=whole(B, lo, n), dst_ref=whole(A, lo, n),
            send_sem=shift_sem.at[k], recv_sem=arrive_sem.at[k],
            device_id=(g + 1, r), device_id_type=MESH,
        )

    def halo(which, lo, n, slot):
        def copy(row_from, row_to, side, device):
            return pltpu.make_async_remote_copy(
                src_ref=field.at[which, pl.ds(lo, n), :, pl.ds(row_from, HALO), :],
                dst_ref=field.at[which, pl.ds(lo, n), :, pl.ds(row_to, HALO), :],
                send_sem=halo_send.at[side, slot], recv_sem=halo_recv.at[side, slot],
                device_id=(g, device), device_id_type=MESH,
            )

        return (
            copy(TOP, TOP + 32, 0, down),
            copy(TOP + 32 - HALO, TOP - HALO, 1, up),
        )

    def wrap(ref, lo, to, n):
        for i in range(n):
            ref[to + i] = ref[lo + i]

    pltpu.make_async_copy(whole(B, 0, cols), whole(B, 0, cols), load_sem.at[0]).wait()
    for copy in halo(B, 0, cols, n_windows):
        copy.start()

    @pl.when(g < groups - 1)
    def _():
        for k in range(n_windows):
            shift(k).start()

    @pl.when(g == 1)
    def _():
        pltpu.make_async_copy(whole(S, 0, cols), whole(S, 0, cols), load_sem.at[1]).wait()
        for copy in halo(S, 0, cols, n_windows + 1):
            copy.start()

    def arrived(k):
        lo, n = chunk(k)
        pltpu.make_async_copy(whole(A, lo, n), whole(A, lo, n), arrive_sem.at[k]).wait()
        for copy in halo(A, lo, n, k):
            copy.start()

    def march(src, base, which, k, steps_out):
        def run(fn):
            lax.fori_loop(0, SPAN, fn, 0, unroll=True)

        def fine(a, abase, b, row, rows):
            def one(i, _):
                b[i, :, pl.ds(row, rows), :] = update(a, abase, i, SPAN, row, rows, FINE)
                return 0

            run(one)

        fine(src, base, w0, TOP - 12, 56)
        fine(w0, 0, w1, TOP - 8, 48)
        fine(w1, 0, w0, TOP - 8, 48)
        fine(w0, 0, w2, TOP - 8, 48)
        steps_out()
        fine(w2, 0, w0, TOP - 8, 48)
        fine(w0, 0, w1, TOP - 4, 40)
        fine(w1, 0, w0, TOP - 4, 40)
        row, rows = TOP - 4, 40

        def last(i, _):
            t = update(w0, 0, i, SPAN, row, rows, FINE)
            rough = update(w2, 0, i, SPAN, row, rows, COARSE)
            tau[which, WIDE * k + i, :, pl.ds(row, rows), :] = jnp.where(which == S, t, t - rough)
            return 0

        lax.fori_loop(1, SPAN - 1, last, 0, unroll=True)

    def window(w, _):
        which = w // n_windows
        k = lax.rem(w, n_windows)

        @pl.when((which == S) & (k == 0))
        def _():
            for copy in halo(S, 0, cols, n_windows + 1):
                copy.wait_recv()
            wrap(field.at[S], 0, cols, 2)

        @pl.when((which == B) & (k == 0))
        def _():
            for copy in halo(B, 0, cols, n_windows):
                copy.wait_recv()
            wrap(field.at[B], 0, cols, 2)

        for q in range(n_windows):
            @pl.when((which == A) & (k == q))
            def _(q=q):
                if q == 0:
                    arrived(0)
                if q < n_windows - 1:
                    arrived(q + 1)
                lo, n = chunk(q)
                for copy in halo(A, lo, n, q):
                    copy.wait_recv()
                if q == n_windows - 1:
                    wrap(field.at[A], 0, cols, 2)

        def steps_out():
            @pl.when(which == A)
            def _():
                def one(i, _):
                    f = WIDE * k + i
                    relaxed[f, :, pl.ds(TOP - 8, 48), :] = w2[i, :, pl.ds(TOP - 8, 48), :]
                    pltpu.make_async_copy(
                        relaxed.at[f, :, strip, :],
                        relaxed_ref.at[:, :, pl.ds(pl.multiple_of((f - 1) * LANES, LANES), LANES)],
                        out_sem.at[0],
                    ).start()
                    return 0

                lax.fori_loop(1, SPAN - 1, one, 0)

        march(field.at[which], WIDE * k, which, k, steps_out)
        return 0

    lax.fori_loop(jnp.where(g == 1, 0, n_windows), 3 * n_windows, window, 0)

    for which in (B, A):
        tau[which, 0] = tau[which, cols]
        for i in range(3):
            tau[which, cols + 1 + i] = tau[which, 1 + i]

    @pl.when(g == 0)
    def _():
        def one(f, _):
            state[f, :, pl.ds(TOP - 8, 48), :] = relaxed[f, :, pl.ds(TOP - 8, 48), :]
            return 0

        lax.fori_loop(1, cols + 1, one, 0)

    @pl.when(g == 1)
    def _():
        def one(f, _):
            state[f, :, pl.ds(TOP - 4, 40), :] = tau[S, f, :, pl.ds(TOP - 4, 40), :]
            return 0

        lax.fori_loop(1, cols + 1, one, 0)

    @pl.when(x == 0)
    def _():
        state[0] = state[cols]
        state[cols + 1] = state[1]

    def group_in(j):
        ref = state.at[pl.ds(GROUP * j, GROUP), :, pl.ds(TOP - EDGE, 32 + 2 * EDGE), :]
        pltpu.make_async_copy(ref, ref, chain_recv.at[j]).wait()

    def put_out(p):
        c = lax.rem(p + x - 1 + cols, cols)
        pltpu.make_async_copy(
            state.at[p, :, strip, :],
            corrected_ref.at[:, :, pl.ds(pl.multiple_of(c * LANES, LANES), LANES)],
            out_sem.at[1],
        ).start()

    def group_out(j):
        def copy(row_from, n, row_to, device):
            return pltpu.make_async_remote_copy(
                src_ref=nxt.at[pl.ds(GROUP * j, GROUP), :, pl.ds(row_from, n), :],
                dst_ref=state.at[pl.ds(GROUP * j, GROUP), :, pl.ds(row_to, n), :],
                send_sem=chain_send.at[j], recv_sem=chain_recv.at[j],
                device_id=(g + 2, device), device_id_type=MESH,
            )

        copy(TOP, EDGE, TOP + 32, down).start()
        copy(TOP + 32 - EDGE, EDGE, TOP - EDGE, up).start()
        copy(TOP, 32, TOP, r).start()

    def chain(j, _):
        @pl.when(x > 0)
        def _():
            @pl.when(j == 0)
            def _():
                group_in(0)
                put_out(0)
                put_out(1)
                for i in range(2):
                    state[cols + i] = state[i]

            @pl.when(j < n_groups - 1)
            def _():
                group_in(j + 1)
                put_out(GROUP * (j + 1))
                put_out(GROUP * (j + 1) + 1)

        @pl.when(x == 0)
        def _():
            put_out(GROUP * j + 1)
            put_out(GROUP * j + 2)

        @pl.when(g < groups - 2)
        def _():
            base = GROUP * j

            def rough(i, _):
                rows = pl.ds(TOP - 4, 40)
                mid[i, :, rows, :] = update(state, base, i, GROUP + 2, TOP - 4, 40, COARSE) + tau[A, base + x + i, :, rows, :]
                return 0

            lax.fori_loop(0, GROUP + 2, rough, 0, unroll=True)

            def rough2(i, _):
                nxt[base + i, :, strip, :] = update(mid, 0, i + 1, GROUP + 2, TOP, 32, COARSE) + tau[B, base + x + 1 + i, :, strip, :]
                return 0

            lax.fori_loop(0, GROUP, rough2, 0, unroll=True)
            group_out(j)

        return 0

    lax.fori_loop(0, n_groups, chain, 0)

    for copy in halo(B, 0, cols, n_windows):
        copy.wait_send()
    for k in range(n_windows):
        lo, n = chunk(k)
        for copy in halo(A, lo, n, k):
            copy.wait_send()

    @pl.when(g == 1)
    def _():
        for copy in halo(S, 0, cols, n_windows + 1):
            copy.wait_send()

    @pl.when(g < groups - 1)
    def _():
        for k in range(n_windows):
            shift(k).wait_send()

    @pl.when(g < groups - 2)
    def _():
        def one(j, _):
            ref = nxt.at[pl.ds(GROUP * j, GROUP), :, pl.ds(TOP, 32 + 2 * EDGE), :]
            pltpu.make_async_copy(ref, ref, chain_send.at[j]).wait()
            return 0

        lax.fori_loop(0, n_groups, one, 0)

    for i in range(2):
        done = relaxed.at[pl.ds(0, cols), :, strip, :]
        pltpu.make_async_copy(done, done, out_sem.at[i]).wait()


def shards(start_state, guess):
    guess = guess[0]
    _, rows, width = guess.shape
    cols = width // LANES
    strips = lax.axis_size("rows")
    groups = lax.axis_size("tm")
    out = jax.ShapeDtypeStruct(guess.shape, guess.dtype)
    n_windows = cols // WIDE
    n_groups = cols // GROUP

    def frames(*lead):
        return pltpu.VMEM((*lead, 2, FRAME, LANES), jnp.float32)

    dma = pltpu.SemaphoreType.DMA
    corrected, relaxed = pl.pallas_call(
        functools.partial(kernel, cols, groups, strips),
        out_shape=(out, out),
        in_specs=[pl.BlockSpec(memory_space=pl.ANY)] * 2,
        out_specs=(pl.BlockSpec(memory_space=pl.ANY),) * 2,
        scratch_shapes=[
            frames(3, cols + 2), frames(3, cols + 4),
            frames(SPAN), frames(SPAN), frames(SPAN),
            frames(cols + 2), frames(cols + 2), frames(GROUP + 2), frames(cols),
            dma((2,)), dma((n_windows,)), dma((n_windows,)),
            dma((2, n_windows + 2)), dma((2, n_windows + 2)),
            dma((n_groups,)), dma((n_groups,)), dma((2,)),
        ],
        compiler_params=pltpu.CompilerParams(
            collective_id=0, has_side_effects=True, vmem_limit_bytes=48 * 2**20
        ),
    )(start_state, guess)
    return corrected[None], relaxed[None]


def solution(mesh):
    return jax.shard_map(
        shards,
        mesh=mesh,
        in_specs=(P(None, "rows", None), P("tm", None, "rows", None)),
        out_specs=(P("tm", None, "rows", None), P("tm", None, "rows", None)),
        check_vma=False,
    )
```

```python
import functools

import jax
import jax.numpy as jnp
from jax import lax
from jax.experimental import pallas as pl
from jax.experimental.pallas import tpu as pltpu
from jax.sharding import PartitionSpec as P

STEPS = 4
FINE = 0.05
COARSE = STEPS * FINE
VISCOSITY = 1.0
MESH = pl.DeviceIdType.MESH

LANES = 128
TOP = 16
FRAME = 64
ROWS = 32
DEEP = 9
SHALLOW = 4
EDGE = 2
WIDE = 8
SPAN = WIDE + 2
GROUP = 2


def update(src, base, i, count, row, rows, size):
    lane = lax.broadcasted_iota(jnp.int32, (2, rows, LANES), 2)
    here = pl.ds(row, rows)
    left = base + jnp.maximum(i - 1, 0)
    right = base + jnp.minimum(i + 1, count - 1)
    c = src[base + i, :, here, :]
    east = pltpu.roll(jnp.where(lane == 0, src[right, :, here, :], c), LANES - 1, 2)
    west = pltpu.roll(jnp.where(lane == LANES - 1, src[left, :, here, :], c), 1, 2)
    upper = src[base + i, :, pl.ds(row + 1, rows), :]
    lower = src[base + i, :, pl.ds(row - 1, rows), :]
    u = (0.5 * size) * c[0:1]
    v = (0.5 * size) * c[1:2]
    k = size * VISCOSITY
    return (1.0 - 4.0 * k) * c + ((k - u) * east + (k + u) * west) + ((k - v) * upper + (k + v) * lower)


def kernel(
    cols, groups, strips, start_ref, guess_ref, corrected_ref, relaxed_ref,
    field, spare, tau, w0, w1, w2, relaxed, state, mid, odd_state, nxt,
    load_sem, arrive_sem, shift_sem, edge_sem, halo_send, halo_recv,
    chain_send, chain_recv, pass_send, out_sem,
):
    g = lax.axis_index("tm")
    r = lax.axis_index("rows")
    x = g // 2
    even = lax.rem(g, 2) == 0
    core = lax.rem(r, 2)
    up = lax.rem(r + 1, strips)
    down = lax.rem(r + strips - 1, strips)
    sibling = r + 1 - 2 * core
    outer = jnp.where(core == 0, down, up)
    n_windows = cols // WIDE
    n_groups = cols // GROUP
    strip = pl.ds(TOP, ROWS)
    B, A = 0, 1
    has_next = g < groups - 1
    has_far = even & (g < groups - 2)

    barrier = pltpu.get_barrier_semaphore()

    def greet(group, row):
        pl.semaphore_signal(barrier, inc=1, device_id=(group, row), device_id_type=MESH)

    greet(g, up)
    greet(g, down)

    @pl.when(g == 0)
    def _():
        greet(1, outer)

    @pl.when(g >= 1)
    def _():
        greet(g - 1, r)
        greet(g - 1, outer)

    @pl.when(even & (g >= 2))
    def _():
        greet(g - 2, r)
        greet(g - 2, up)
        greet(g - 2, down)

    def chunk(k):
        if k == 0:
            return 0, SPAN
        if k < n_windows - 1:
            return WIDE * k + 2, WIDE
        return WIDE * k + 2, WIDE - 2

    def load(src, dst, sems):
        for k in range(n_windows):
            lo, n = chunk(k)

            def one(f, _, k=k):
                c = lax.rem(f + cols - 1, cols)
                pltpu.make_async_copy(
                    src.at[:, :, pl.ds(pl.multiple_of(c * LANES, LANES), LANES)],
                    dst.at[f, :, strip, :],
                    sems.at[k],
                ).start()
                return 0

            lax.fori_loop(lo, lo + n, one, 0)

    load(guess_ref, field.at[B], load_sem.at[0])

    @pl.when(g == 0)
    def _():
        load(start_ref, field.at[A], arrive_sem)

    @pl.when(g == 1)
    def _():
        load(start_ref, spare, load_sem.at[1])

    pl.semaphore_wait(
        barrier,
        2 + jnp.where(has_next, 2, 0) + jnp.where(g == 1, 1, 0) + jnp.where(has_far, 3, 0),
    )

    def rows_of(ref, lo, n, row, count):
        return ref.at[pl.ds(lo, n), :, pl.ds(row, count), :]

    def await_bytes(ref, sem):
        pltpu.make_async_copy(ref, ref, sem).wait()

    def sides(src, dst, lo, n, depth, send, recv, group, device, side):
        row_from, row_to = ((TOP, TOP + ROWS), (TOP + ROWS - depth, TOP - depth))[side]
        return pltpu.make_async_remote_copy(
            src_ref=rows_of(src, lo, n, row_from, depth), dst_ref=rows_of(dst, lo, n, row_to, depth),
            send_sem=send, recv_sem=recv, device_id=(group, device), device_id_type=MESH,
        )

    def shift(k):
        lo, n = chunk(k)
        return pltpu.make_async_remote_copy(
            src_ref=rows_of(field.at[B], lo, n, TOP, ROWS), dst_ref=rows_of(field.at[A], lo, n, TOP, ROWS),
            send_sem=shift_sem.at[k], recv_sem=arrive_sem.at[k],
            device_id=(g + 1, r), device_id_type=MESH,
        )

    def inner(which, k, depth):
        lo, n = chunk(k)
        f = field.at[which]
        return [
            (core == 1 - side, sides(f, f, lo, n, depth, halo_send.at[which, 0, k], halo_recv.at[which, 0, k], g, sibling, side))
            for side in (0, 1)
        ]

    def outside(k):
        lo, n = chunk(k)
        f = field.at[B]
        return [
            (core == side, sides(f, f, lo, n, DEEP, halo_send.at[B, 1, k], halo_recv.at[B, 1, k], g, outer, side))
            for side in (0, 1)
        ]

    def onward(k, depth):
        lo, n = chunk(k)
        return [
            (core == side, sides(field.at[B], field.at[A], lo, n, depth, edge_sem.at[k], arrive_sem.at[k], g + 1, outer, side))
            for side in (0, 1)
        ]

    def back(k):
        lo, n = chunk(k)
        return [
            (core == side, sides(spare, field.at[A], lo, n, DEEP, edge_sem.at[n_windows + k], arrive_sem.at[k], 0, outer, side))
            for side in (0, 1)
        ]

    def each(copies, method):
        for condition, copy in copies:
            pl.when(condition)(getattr(copy, method))

    def got(which, side, k, depth):
        lo, n = chunk(k)
        await_bytes(rows_of(field.at[which], lo, n, TOP, depth), halo_recv.at[which, side, k])

    for k in range(n_windows):
        lo, n = chunk(k)
        await_bytes(rows_of(field.at[B], lo, n, TOP, ROWS), load_sem.at[0, k])

        @pl.when(has_far)
        def _(k=k):
            each(outside(k), "start")
            each(inner(B, k, DEEP), "start")

        @pl.when(has_next & even)
        def _(k=k):
            each(onward(k, SHALLOW), "start")
            shift(k).start()

        @pl.when(has_next & ~even)
        def _(k=k):
            each(onward(k, DEEP), "start")
            shift(k).start()

        @pl.when(g == 1)
        def _(k=k):
            await_bytes(rows_of(spare, lo, n, TOP, ROWS), load_sem.at[1, k])
            each(back(k), "start")

    def arrived(k):
        lo, n = chunk(k)

        @pl.when(even)
        def _():
            await_bytes(rows_of(field.at[A], lo, n, TOP, ROWS + DEEP), arrive_sem.at[k])
            each(inner(A, k, DEEP), "start")

        @pl.when(~even)
        def _():
            await_bytes(rows_of(field.at[A], lo, n, TOP, ROWS + SHALLOW), arrive_sem.at[k])
            each(inner(A, k, SHALLOW), "start")

    def wrap(ref, lo, to, n):
        for i in range(n):
            ref[to + i] = ref[lo + i]

    def march(which, k):
        src, base = field.at[which], WIDE * k

        def fine(a, abase, b, row, rows):
            def one(i, _):
                b[i, :, pl.ds(row, rows), :] = update(a, abase, i, SPAN, row, rows, FINE)
                return 0

            lax.fori_loop(0, SPAN, one, 0, unroll=True)

        fine(src, base, w0, TOP - 8, 48)
        fine(w0, 0, w1, TOP - 8, 48)
        fine(w1, 0, w0, TOP - 8, 48)
        fine(w0, 0, w2, TOP - 8, 48)

        @pl.when(which == A)
        def _():
            def one(i, _):
                f = base + i
                there = pl.ds(pl.multiple_of((f - 1) * LANES, LANES), LANES)
                relaxed[f, :, strip, :] = w2[i, :, strip, :]
                pltpu.make_async_copy(relaxed.at[f, :, strip, :], relaxed_ref.at[:, :, there], out_sem.at[0]).start()

                @pl.when(g == 0)
                def _():
                    pltpu.make_async_copy(relaxed.at[f, :, strip, :], corrected_ref.at[:, :, there], out_sem.at[1]).start()

                return 0

            lax.fori_loop(1, SPAN - 1, one, 0)

        @pl.when(even)
        def _():
            row, rows = TOP - 4, 40
            fine(w2, 0, w0, row, rows)
            fine(w0, 0, w1, row, rows)
            fine(w1, 0, w0, row, rows)

            def last(i, _):
                t = update(w0, 0, i, SPAN, row, rows, FINE)
                rough = update(w2, 0, i, SPAN, row, rows, COARSE)
                tau[which, base + i, :, pl.ds(row, rows), :] = jnp.where((g == 0) & (which == A), t, t - rough)
                return 0

            lax.fori_loop(1, SPAN - 1, last, 0, unroll=True)

    def window(w, _):
        k = w // 2
        which = lax.rem(w, 2)
        for q in range(n_windows):
            @pl.when((which == B) & (k == q) & has_far)
            def _(q=q):
                got(B, 0, q, DEEP)
                got(B, 1, q, DEEP)
                if q == n_windows - 1:
                    wrap(field.at[B], 0, cols, 2)

            @pl.when((which == A) & (k == q))
            def _(q=q):
                if q == 0:
                    arrived(0)
                if q < n_windows - 1:
                    arrived(q + 1)

                @pl.when(even)
                def _():
                    got(A, 0, q, DEEP)

                @pl.when(~even)
                def _():
                    got(A, 0, q, SHALLOW)

                if q == n_windows - 1:
                    wrap(field.at[A], 0, cols, 2)

        @pl.when((which == A) | has_far)
        def _():
            march(which, k)

        return 0

    def put_out(ref, p, offset):
        c = lax.rem(p + offset, cols)
        pltpu.make_async_copy(
            ref.at[p, :, strip, :],
            corrected_ref.at[:, :, pl.ds(pl.multiple_of(c * LANES, LANES), LANES)],
            out_sem.at[1],
        ).start()

    def group_in(j, extra):
        await_bytes(rows_of(state, GROUP * j, GROUP, TOP - extra, ROWS + 2 * extra), chain_recv.at[j])

    def group_out(j):
        def copy(row_from, n, row_to, device):
            return pltpu.make_async_remote_copy(
                src_ref=rows_of(nxt, GROUP * j, GROUP, row_from, n),
                dst_ref=rows_of(state, GROUP * j, GROUP, row_to, n),
                send_sem=chain_send.at[j], recv_sem=chain_recv.at[j],
                device_id=(g + 2, device), device_id_type=MESH,
            )

        copy(TOP, EDGE, TOP + ROWS, down).start()
        copy(TOP + ROWS - EDGE, EDGE, TOP - EDGE, up).start()
        copy(TOP, ROWS, TOP, r).start()

    def pass_on(j):
        return pltpu.make_async_remote_copy(
            src_ref=rows_of(odd_state, GROUP * j, GROUP, TOP, ROWS),
            dst_ref=rows_of(state, GROUP * j, GROUP, TOP, ROWS),
            send_sem=pass_send.at[j], recv_sem=chain_recv.at[j],
            device_id=(g + 1, r), device_id_type=MESH,
        )

    def chain(j, _):
        base = GROUP * j
        row, rows = TOP - 4, 40

        @pl.when(x > 0)
        def _():
            @pl.when(j == 0)
            def _():
                group_in(0, EDGE)
                wrap(state, 0, cols, 2)
                for i in range(GROUP):
                    put_out(state, i, x)

            @pl.when(j < n_groups - 1)
            def _():
                group_in(j + 1, EDGE)
                for i in range(GROUP):
                    put_out(state, GROUP * (j + 1) + i, x)

            def rough(i, _):
                mid[i, :, pl.ds(row, rows), :] = update(state, base, i, GROUP + 2, row, rows, COARSE) + tau[A, base + x + 1 + i, :, pl.ds(row, rows), :]
                return 0

            lax.fori_loop(0, GROUP + 2, rough, 0, unroll=True)

        @pl.when(x == 0)
        def _():
            def same(i, _):
                mid[i, :, pl.ds(row, rows), :] = tau[A, base + 1 + i, :, pl.ds(row, rows), :]
                return 0

            lax.fori_loop(0, GROUP + 2, same, 0, unroll=True)

        for i in range(GROUP):
            odd_state[base + i, :, strip, :] = mid[1 + i, :, strip, :]

        @pl.when(has_far)
        def _():
            def rough(i, _):
                nxt[base + i, :, strip, :] = update(mid, 0, i + 1, GROUP + 2, TOP, ROWS, COARSE) + tau[B, base + x + 2 + i, :, strip, :]
                return 0

            lax.fori_loop(0, GROUP, rough, 0, unroll=True)
            group_out(j)

        pass_on(j).start()
        return 0

    ahead = WIDE // GROUP

    def rounds(k, _):
        @pl.when(k < n_windows)
        def _():
            lax.fori_loop(2 * k, 2 * k + 2, window, 0)

        @pl.when(k == n_windows)
        def _():
            for which in (B, A):
                for i in range(5):
                    tau[which, cols + 1 + i] = tau[which, 1 + i]

        @pl.when(even)
        def _():
            first = jnp.maximum(ahead * (k - 1 - x) + 2, 0)
            stop = jnp.maximum(ahead * (k - x) + 2, 0)
            lax.fori_loop(first, jnp.where(k == n_windows, n_groups, stop), chain, 0)

        return 0

    lax.fori_loop(0, n_windows + 1, rounds, 0)

    @pl.when(~even)
    def _():
        def one(j, _):
            group_in(j, 0)
            for i in range(GROUP):
                put_out(state, GROUP * j + i, x + 1)
            return 0

        lax.fori_loop(0, n_groups, one, 0)

    for k in range(n_windows):
        @pl.when(has_far)
        def _(k=k):
            each(outside(k), "wait_send")
            each(inner(B, k, DEEP), "wait_send")

        @pl.when(has_next & even)
        def _(k=k):
            each(onward(k, SHALLOW), "wait_send")

        @pl.when(has_next & ~even)
        def _(k=k):
            each(onward(k, DEEP), "wait_send")

        @pl.when(has_next)
        def _(k=k):
            shift(k).wait_send()

        @pl.when(even)
        def _(k=k):
            each(inner(A, k, DEEP), "wait_send")

        @pl.when(~even)
        def _(k=k):
            each(inner(A, k, SHALLOW), "wait_send")

        @pl.when(g == 1)
        def _(k=k):
            each(back(k), "wait_send")

    @pl.when(even)
    def _():
        def one(j, _):
            pass_on(j).wait_send()

            @pl.when(has_far)
            def _():
                await_bytes(rows_of(nxt, GROUP * j, GROUP, TOP, ROWS + 2 * EDGE), chain_send.at[j])

            return 0

        lax.fori_loop(0, n_groups, one, 0)

    for i in range(2):
        await_bytes(rows_of(relaxed, 1, cols, TOP, ROWS), out_sem.at[i])


def shards(start_state, guess):
    guess = guess[0]
    width = guess.shape[2]
    cols = width // LANES
    strips = lax.axis_size("rows")
    groups = lax.axis_size("tm")
    out = jax.ShapeDtypeStruct(guess.shape, guess.dtype)
    n_windows = cols // WIDE
    n_groups = cols // GROUP

    def frames(*lead):
        return pltpu.VMEM((*lead, 2, FRAME, LANES), jnp.float32)

    dma = pltpu.SemaphoreType.DMA
    corrected, relaxed = pl.pallas_call(
        functools.partial(kernel, cols, groups, strips),
        out_shape=(out, out),
        in_specs=[pl.BlockSpec(memory_space=pl.ANY)] * 2,
        out_specs=(pl.BlockSpec(memory_space=pl.ANY),) * 2,
        scratch_shapes=[
            frames(2, cols + 2), frames(cols), frames(2, cols + 6),
            frames(SPAN), frames(SPAN), frames(SPAN),
            frames(cols + 1), frames(cols + 2), frames(GROUP + 2), frames(cols), frames(cols),
            dma((2, n_windows)), dma((n_windows,)), dma((n_windows,)), dma((2 * n_windows,)),
            dma((2, 2, n_windows)), dma((2, 2, n_windows)),
            dma((n_groups,)), dma((n_groups,)), dma((n_groups,)), dma((2,)),
        ],
        compiler_params=pltpu.CompilerParams(
            collective_id=0, has_side_effects=True, vmem_limit_bytes=62 * 2**20
        ),
    )(start_state, guess)
    return corrected[None], relaxed[None]


def solution(mesh):
    return jax.shard_map(
        shards,
        mesh=mesh,
        in_specs=(P(None, "rows", None), P("tm", None, "rows", None)),
        out_specs=(P("tm", None, "rows", None), P("tm", None, "rows", None)),
        check_vma=False,
    )
```

```python
import functools

import jax
import jax.numpy as jnp
from jax import lax
from jax.experimental import pallas as pl
from jax.experimental.pallas import tpu as pltpu
from jax.sharding import PartitionSpec as P

STEPS = 4
FINE = 0.05
COARSE = STEPS * FINE
VISCOSITY = 1.0
MESH = pl.DeviceIdType.MESH

LANES = 128
TOP = 16
FRAME = 64
ROWS = 32
DEEP = 9
OWN = 8
SHALLOW = 4
EDGE = 2
WIDE = 4
SPAN = WIDE + 2
GROUP = 2


def update(src, base, i, count, row, rows, size):
    lane = lax.broadcasted_iota(jnp.int32, (2, rows, LANES), 2)
    here = pl.ds(row, rows)
    left = base + jnp.maximum(i - 1, 0)
    right = base + jnp.minimum(i + 1, count - 1)
    c = src[base + i, :, here, :]
    east = pltpu.roll(jnp.where(lane == 0, src[right, :, here, :], c), LANES - 1, 2)
    west = pltpu.roll(jnp.where(lane == LANES - 1, src[left, :, here, :], c), 1, 2)
    upper = src[base + i, :, pl.ds(row + 1, rows), :]
    lower = src[base + i, :, pl.ds(row - 1, rows), :]
    u = (0.5 * size) * c[0:1]
    v = (0.5 * size) * c[1:2]
    k = size * VISCOSITY
    return (1.0 - 4.0 * k) * c + ((k - u) * east + (k + u) * west) + ((k - v) * upper + (k + v) * lower)


def kernel(
    cols, groups, strips, start_ref, guess_ref, corrected_ref, relaxed_ref,
    field, spare, tau, w0, w1, w2, relaxed, state, mid, odd_state, nxt,
    load_sem, arrive_sem, shift_sem, edge_sem, halo_send, halo_recv,
    chain_send, chain_recv, pass_send, out_sem,
):
    g = lax.axis_index("tm")
    r = lax.axis_index("rows")
    x = g // 2
    even = lax.rem(g, 2) == 0
    core = lax.rem(r, 2)
    up = lax.rem(r + 1, strips)
    down = lax.rem(r + strips - 1, strips)
    sibling = r + 1 - 2 * core
    outer = jnp.where(core == 0, down, up)
    n_windows = cols // WIDE
    n_groups = cols // GROUP
    strip = pl.ds(TOP, ROWS)
    B, A = 0, 1
    has_next = g < groups - 1
    has_far = even & (g < groups - 2)

    barrier = pltpu.get_barrier_semaphore()

    def greet(group, row):
        pl.semaphore_signal(barrier, inc=1, device_id=(group, row), device_id_type=MESH)

    greet(g, up)
    greet(g, down)

    @pl.when(g == 0)
    def _():
        greet(1, outer)

    @pl.when(g >= 1)
    def _():
        greet(g - 1, r)
        greet(g - 1, outer)

    @pl.when(even & (g >= 2))
    def _():
        greet(g - 2, r)
        greet(g - 2, up)
        greet(g - 2, down)

    def chunk(k):
        if k == 0:
            return 0, SPAN
        if k < n_windows - 1:
            return WIDE * k + 2, WIDE
        return WIDE * k + 2, WIDE - 2

    def load(src, dst, sems):
        for k in range(n_windows):
            lo, n = chunk(k)

            def one(f, _, k=k):
                c = lax.rem(f + cols - 1, cols)
                pltpu.make_async_copy(
                    src.at[:, :, pl.ds(pl.multiple_of(c * LANES, LANES), LANES)],
                    dst.at[f, :, strip, :],
                    sems.at[k],
                ).start()
                return 0

            lax.fori_loop(lo, lo + n, one, 0)

    load(guess_ref, field.at[B], load_sem.at[0])

    @pl.when(g == 0)
    def _():
        load(start_ref, field.at[A], arrive_sem)

    @pl.when(g == 1)
    def _():
        load(start_ref, spare, load_sem.at[1])

    pl.semaphore_wait(
        barrier,
        2 + jnp.where(has_next, 2, 0) + jnp.where(g == 1, 1, 0) + jnp.where(has_far, 3, 0),
    )

    def rows_of(ref, lo, n, row, count):
        return ref.at[pl.ds(lo, n), :, pl.ds(row, count), :]

    def await_bytes(ref, sem):
        pltpu.make_async_copy(ref, ref, sem).wait()

    def sides(src, dst, lo, n, depth, send, recv, group, device, side):
        row_from, row_to = ((TOP, TOP + ROWS), (TOP + ROWS - depth, TOP - depth))[side]
        return pltpu.make_async_remote_copy(
            src_ref=rows_of(src, lo, n, row_from, depth), dst_ref=rows_of(dst, lo, n, row_to, depth),
            send_sem=send, recv_sem=recv, device_id=(group, device), device_id_type=MESH,
        )

    def shift(k):
        lo, n = chunk(k)
        return pltpu.make_async_remote_copy(
            src_ref=rows_of(field.at[B], lo, n, TOP, ROWS), dst_ref=rows_of(field.at[A], lo, n, TOP, ROWS),
            send_sem=shift_sem.at[k], recv_sem=arrive_sem.at[k],
            device_id=(g + 1, r), device_id_type=MESH,
        )

    def inner(which, k, depth):
        lo, n = chunk(k)
        f = field.at[which]
        return [
            (core == 1 - side, sides(f, f, lo, n, depth, halo_send.at[which, 0, k], halo_recv.at[which, 0, k], g, sibling, side))
            for side in (0, 1)
        ]

    def outside(k):
        lo, n = chunk(k)
        f = field.at[B]
        return [
            (core == side, sides(f, f, lo, n, OWN, halo_send.at[B, 1, k], halo_recv.at[B, 1, k], g, outer, side))
            for side in (0, 1)
        ]

    def onward(k, depth):
        lo, n = chunk(k)
        return [
            (core == side, sides(field.at[B], field.at[A], lo, n, depth, edge_sem.at[k], arrive_sem.at[k], g + 1, outer, side))
            for side in (0, 1)
        ]

    def back(k):
        lo, n = chunk(k)
        return [
            (core == side, sides(spare, field.at[A], lo, n, DEEP, edge_sem.at[n_windows + k], arrive_sem.at[k], 0, outer, side))
            for side in (0, 1)
        ]

    def each(copies, method):
        for condition, copy in copies:
            pl.when(condition)(getattr(copy, method))

    def got(which, side, k, depth):
        lo, n = chunk(k)
        await_bytes(rows_of(field.at[which], lo, n, TOP, depth), halo_recv.at[which, side, k])

    @pl.when(g == 1)
    def _():
        for k in range(n_windows):
            lo, n = chunk(k)
            await_bytes(rows_of(spare, lo, n, TOP, ROWS), load_sem.at[1, k])
            each(back(k), "start")

    for k in range(n_windows):
        lo, n = chunk(k)
        await_bytes(rows_of(field.at[B], lo, n, TOP, ROWS), load_sem.at[0, k])

        @pl.when(has_far)
        def _(k=k):
            each(outside(k), "start")
            each(inner(B, k, OWN), "start")

        @pl.when(has_next & even)
        def _(k=k):
            each(onward(k, SHALLOW), "start")
            shift(k).start()

        @pl.when(has_next & ~even)
        def _(k=k):
            each(onward(k, DEEP), "start")
            shift(k).start()

    def arrived(k):
        lo, n = chunk(k)

        @pl.when(even)
        def _():
            await_bytes(rows_of(field.at[A], lo, n, TOP, ROWS + DEEP), arrive_sem.at[k])
            each(inner(A, k, DEEP), "start")

        @pl.when(~even)
        def _():
            await_bytes(rows_of(field.at[A], lo, n, TOP, ROWS + SHALLOW), arrive_sem.at[k])
            each(inner(A, k, SHALLOW), "start")

    def wrap(ref, lo, to, n):
        for i in range(n):
            ref[to + i] = ref[lo + i]

    def fine(a, abase, b, row, rows):
        def one(i, _):
            b[i, :, pl.ds(row, rows), :] = update(a, abase, i, SPAN, row, rows, FINE)
            return 0

        lax.fori_loop(0, SPAN, one, 0, unroll=True)

    def excess(which, k, row, rows, rough):
        def one(i, _):
            t = update(w0, 0, i, SPAN, row, rows, FINE)
            if rough:
                t = t - update(w2, 0, i, SPAN, row, rows, COARSE)
            tau[which, WIDE * k + i, :, pl.ds(row, rows), :] = t
            return 0

        lax.fori_loop(1, SPAN - 1, one, 0, unroll=True)

    def march_own(k):
        for q in range(n_windows):
            @pl.when(k == q)
            def _(q=q):
                got(B, 0, q, OWN)
                got(B, 1, q, OWN)
                if q == n_windows - 1:
                    wrap(field.at[B], 0, cols, 2)

        fine(field.at[B], WIDE * k, w0, TOP - 8, 48)
        fine(w0, 0, w1, TOP - 8, 48)
        fine(w1, 0, w0, TOP - 8, 48)
        fine(w0, 0, w2, TOP - 4, 40)
        fine(w2, 0, w0, TOP - 4, 40)
        fine(w0, 0, w1, TOP - 4, 40)
        fine(w1, 0, w0, TOP - 4, 40)
        excess(B, k, TOP, ROWS, True)

    def march_prior(k):
        for q in range(n_windows):
            @pl.when(k == q)
            def _(q=q):
                @pl.when(even)
                def _():
                    got(A, 0, q, DEEP)

                @pl.when(~even)
                def _():
                    got(A, 0, q, SHALLOW)

                if q == n_windows - 1:
                    wrap(field.at[A], 0, cols, 2)

        base = WIDE * k
        fine(field.at[A], base, w0, TOP - 8, 48)
        fine(w0, 0, w1, TOP - 8, 48)
        fine(w1, 0, w0, TOP - 8, 48)
        fine(w0, 0, w2, TOP - 8, 48)

        def put(i, _):
            f = base + i
            there = pl.ds(pl.multiple_of((f - 1) * LANES, LANES), LANES)
            relaxed[f, :, strip, :] = w2[i, :, strip, :]
            pltpu.make_async_copy(relaxed.at[f, :, strip, :], relaxed_ref.at[:, :, there], out_sem.at[0]).start()

            @pl.when(g == 0)
            def _():
                pltpu.make_async_copy(relaxed.at[f, :, strip, :], corrected_ref.at[:, :, there], out_sem.at[1]).start()

            return 0

        lax.fori_loop(1, SPAN - 1, put, 0)

        @pl.when(even)
        def _():
            row, rows = TOP - 4, 40
            fine(w2, 0, w0, row, rows)
            fine(w0, 0, w1, row, rows)
            fine(w1, 0, w0, row, rows)

            @pl.when(g == 0)
            def _():
                excess(A, k, row, rows, False)

            @pl.when(g > 0)
            def _():
                excess(A, k, row, rows, True)

    def put_out(ref, p, offset):
        c = lax.rem(p + offset, cols)
        pltpu.make_async_copy(
            ref.at[p, :, strip, :],
            corrected_ref.at[:, :, pl.ds(pl.multiple_of(c * LANES, LANES), LANES)],
            out_sem.at[1],
        ).start()

    def group_in(j, extra):
        await_bytes(rows_of(state, GROUP * j, GROUP, TOP - extra, ROWS + 2 * extra), chain_recv.at[j])

    def group_out(j):
        def copy(row_from, n, row_to, device):
            return pltpu.make_async_remote_copy(
                src_ref=rows_of(nxt, GROUP * j, GROUP, row_from, n),
                dst_ref=rows_of(state, GROUP * j, GROUP, row_to, n),
                send_sem=chain_send.at[j], recv_sem=chain_recv.at[j],
                device_id=(g + 2, device), device_id_type=MESH,
            )

        copy(TOP, EDGE, TOP + ROWS, down).start()
        copy(TOP + ROWS - EDGE, EDGE, TOP - EDGE, up).start()
        copy(TOP, ROWS, TOP, r).start()

    def pass_on(j, src, first):
        return pltpu.make_async_remote_copy(
            src_ref=rows_of(src, first, GROUP, TOP, ROWS),
            dst_ref=rows_of(state, GROUP * j, GROUP, TOP, ROWS),
            send_sem=pass_send.at[j], recv_sem=chain_recv.at[j],
            device_id=(g + 1, r), device_id_type=MESH,
        )

    def chain(j, _):
        base = GROUP * j
        row, rows = TOP - 4, 40

        def onward_state(src, first):
            def rough(i, _):
                nxt[base + i, :, strip, :] = update(src, first, i + 1, GROUP + 2, TOP, ROWS, COARSE) + tau[B, base + x + 2 + i, :, strip, :]
                return 0

            lax.fori_loop(0, GROUP, rough, 0, unroll=True)
            group_out(j)

        @pl.when(x > 0)
        def _():
            @pl.when(j == 0)
            def _():
                group_in(0, EDGE)
                wrap(state, 0, cols, 2)
                for i in range(GROUP):
                    put_out(state, i, x)

            @pl.when(j < n_groups - 1)
            def _():
                group_in(j + 1, EDGE)
                for i in range(GROUP):
                    put_out(state, GROUP * (j + 1) + i, x)

            def rough(i, _):
                mid[i, :, pl.ds(row, rows), :] = update(state, base, i, GROUP + 2, row, rows, COARSE) + tau[A, base + x + 1 + i, :, pl.ds(row, rows), :]
                return 0

            lax.fori_loop(0, GROUP + 2, rough, 0, unroll=True)

            @pl.when(has_far)
            def _():
                onward_state(mid, 0)

            for i in range(GROUP):
                odd_state[base + i, :, strip, :] = mid[1 + i, :, strip, :]
            pass_on(j, odd_state, base).start()

        @pl.when(x == 0)
        def _():
            onward_state(tau.at[A], base + 1)
            pass_on(j, tau.at[A], base + 2).start()

        return 0

    ahead = WIDE // GROUP
    lead = jnp.where(x == 0, 0, 2)

    def rounds(k, _):
        now = (k >= 0) & (k < n_windows)
        for q in range(n_windows):
            @pl.when(k == q)
            def _(q=q):
                arrived(q)

        @pl.when(has_far & (k + lead < n_windows))
        def _():
            march_own(k + lead)

        @pl.when(now)
        def _():
            march_prior(k)

        @pl.when(k == n_windows)
        def _():
            for which in (B, A):
                for i in range(5):
                    tau[which, cols + 1 + i] = tau[which, 1 + i]

        @pl.when(even)
        def _():
            first = jnp.maximum(ahead * (k - 1) + 1 - x, 0)
            stop = jnp.maximum(ahead * k + 1 - x, 0)
            lax.fori_loop(first, jnp.where(k == n_windows, n_groups, stop), chain, 0)

        return 0

    lax.fori_loop(-lead, n_windows + 1, rounds, 0)

    @pl.when(~even)
    def _():
        def one(j, _):
            group_in(j, 0)
            for i in range(GROUP):
                put_out(state, GROUP * j + i, x + 1)
            return 0

        lax.fori_loop(0, n_groups, one, 0)

    for k in range(n_windows):
        @pl.when(has_far)
        def _(k=k):
            each(outside(k), "wait_send")
            each(inner(B, k, OWN), "wait_send")

        @pl.when(has_next & even)
        def _(k=k):
            each(onward(k, SHALLOW), "wait_send")

        @pl.when(has_next & ~even)
        def _(k=k):
            each(onward(k, DEEP), "wait_send")

        @pl.when(has_next)
        def _(k=k):
            shift(k).wait_send()

        @pl.when(even)
        def _(k=k):
            each(inner(A, k, DEEP), "wait_send")

        @pl.when(~even)
        def _(k=k):
            each(inner(A, k, SHALLOW), "wait_send")

        @pl.when(g == 1)
        def _(k=k):
            each(back(k), "wait_send")

    @pl.when(even)
    def _():
        def one(j, _):
            pass_on(j, odd_state, 0).wait_send()

            @pl.when(has_far)
            def _():
                await_bytes(rows_of(nxt, GROUP * j, GROUP, TOP, ROWS + 2 * EDGE), chain_send.at[j])

            return 0

        lax.fori_loop(0, n_groups, one, 0)

    for i in range(2):
        await_bytes(rows_of(relaxed, 1, cols, TOP, ROWS), out_sem.at[i])


def shards(start_state, guess):
    guess = guess[0]
    width = guess.shape[2]
    cols = width // LANES
    strips = lax.axis_size("rows")
    groups = lax.axis_size("tm")
    out = jax.ShapeDtypeStruct(guess.shape, guess.dtype)
    n_windows = cols // WIDE
    n_groups = cols // GROUP

    def frames(*lead):
        return pltpu.VMEM((*lead, 2, FRAME, LANES), jnp.float32)

    dma = pltpu.SemaphoreType.DMA
    corrected, relaxed = pl.pallas_call(
        functools.partial(kernel, cols, groups, strips),
        out_shape=(out, out),
        in_specs=[pl.BlockSpec(memory_space=pl.ANY)] * 2,
        out_specs=(pl.BlockSpec(memory_space=pl.ANY),) * 2,
        scratch_shapes=[
            frames(2, cols + 2), frames(cols), frames(2, cols + 6),
            frames(SPAN), frames(SPAN), frames(SPAN),
            frames(cols + 1), frames(cols + 2), frames(GROUP + 2), frames(cols), frames(cols),
            dma((2, n_windows)), dma((n_windows,)), dma((n_windows,)), dma((2 * n_windows,)),
            dma((2, 2, n_windows)), dma((2, 2, n_windows)),
            dma((n_groups,)), dma((n_groups,)), dma((n_groups,)), dma((2,)),
        ],
        compiler_params=pltpu.CompilerParams(
            collective_id=0, has_side_effects=True, vmem_limit_bytes=61 * 2**20
        ),
    )(start_state, guess)
    return corrected[None], relaxed[None]


def solution(mesh):
    return jax.shard_map(
        shards,
        mesh=mesh,
        in_specs=(P(None, "rows", None), P("tm", None, "rows", None)),
        out_specs=(P("tm", None, "rows", None), P("tm", None, "rows", None)),
        check_vma=False,
    )
```

```python
import functools

import jax
import jax.numpy as jnp
from jax import lax
from jax.experimental import pallas as pl
from jax.experimental.pallas import tpu as pltpu
from jax.sharding import PartitionSpec as P

STEPS = 4
FINE = 0.05
COARSE = STEPS * FINE
VISCOSITY = 1.0
MESH = pl.DeviceIdType.MESH

LANES = 128
TOP = 16
FRAME = 64
ROWS = 32
DEEP = 9
OWN = 8
SHALLOW = 4
EDGE = 2
WIDE = 4
SPAN = WIDE + 2
BROAD = 4
GROUP = 2


def update(src, base, i, count, row, rows, size):
    lane = lax.broadcasted_iota(jnp.int32, (2, rows, LANES), 2)
    here = pl.ds(row, rows)
    left = base + jnp.maximum(i - 1, 0)
    right = base + jnp.minimum(i + 1, count - 1)
    c = src[base + i, :, here, :]
    east = pltpu.roll(jnp.where(lane == 0, src[right, :, here, :], c), LANES - 1, 2)
    west = pltpu.roll(jnp.where(lane == LANES - 1, src[left, :, here, :], c), 1, 2)
    upper = src[base + i, :, pl.ds(row + 1, rows), :]
    lower = src[base + i, :, pl.ds(row - 1, rows), :]
    u = (0.5 * size) * c[0:1]
    v = (0.5 * size) * c[1:2]
    k = size * VISCOSITY
    return (1.0 - 4.0 * k) * c + ((k - u) * east + (k + u) * west) + ((k - v) * upper + (k + v) * lower)


def kernel(
    cols, groups, strips, start_ref, guess_ref, corrected_ref, relaxed_ref,
    field, spare, tau, steps, relaxed, state, mid, odd_state, nxt,
    load_sem, arrive_sem, shift_sem, edge_sem, halo_send, halo_recv,
    chain_send, chain_recv, pass_send, out_sem,
):
    g = lax.axis_index("tm")
    r = lax.axis_index("rows")
    x = g // 2
    even = lax.rem(g, 2) == 0
    core = lax.rem(r, 2)
    up = lax.rem(r + 1, strips)
    down = lax.rem(r + strips - 1, strips)
    sibling = r + 1 - 2 * core
    outer = jnp.where(core == 0, down, up)
    n_windows = cols // WIDE
    n_groups = cols // GROUP
    strip = pl.ds(TOP, ROWS)
    B, A = 0, 1
    has_next = g < groups - 1
    has_far = even & (g < groups - 2)

    barrier = pltpu.get_barrier_semaphore()

    def greet(group, row):
        pl.semaphore_signal(barrier, inc=1, device_id=(group, row), device_id_type=MESH)

    greet(g, up)
    greet(g, down)

    @pl.when(g == 0)
    def _():
        greet(1, outer)

    @pl.when(g >= 1)
    def _():
        greet(g - 1, r)
        greet(g - 1, outer)

    @pl.when(even & (g >= 2))
    def _():
        greet(g - 2, r)
        greet(g - 2, up)
        greet(g - 2, down)

    def chunk(k):
        if k == 0:
            return 0, SPAN
        if k < n_windows - 1:
            return WIDE * k + 2, WIDE
        return WIDE * k + 2, WIDE - 2

    def load(src, dst, sems):
        for k in range(n_windows):
            lo, n = chunk(k)

            def one(f, _, k=k):
                c = lax.rem(f + cols - 1, cols)
                pltpu.make_async_copy(
                    src.at[:, :, pl.ds(pl.multiple_of(c * LANES, LANES), LANES)],
                    dst.at[f, :, strip, :],
                    sems.at[k],
                ).start()
                return 0

            lax.fori_loop(lo, lo + n, one, 0)

    load(guess_ref, field.at[B], load_sem.at[0])

    @pl.when(g == 0)
    def _():
        load(start_ref, field.at[A], arrive_sem)

    @pl.when(g == 1)
    def _():
        load(start_ref, spare, load_sem.at[1])

    pl.semaphore_wait(
        barrier,
        2 + jnp.where(has_next, 2, 0) + jnp.where(g == 1, 1, 0) + jnp.where(has_far, 3, 0),
    )

    def rows_of(ref, lo, n, row, count):
        return ref.at[pl.ds(lo, n), :, pl.ds(row, count), :]

    def await_bytes(ref, sem):
        pltpu.make_async_copy(ref, ref, sem).wait()

    def sides(src, dst, lo, n, depth, send, recv, group, device, side):
        row_from, row_to = ((TOP, TOP + ROWS), (TOP + ROWS - depth, TOP - depth))[side]
        return pltpu.make_async_remote_copy(
            src_ref=rows_of(src, lo, n, row_from, depth), dst_ref=rows_of(dst, lo, n, row_to, depth),
            send_sem=send, recv_sem=recv, device_id=(group, device), device_id_type=MESH,
        )

    def shift(k):
        lo, n = chunk(k)
        return pltpu.make_async_remote_copy(
            src_ref=rows_of(field.at[B], lo, n, TOP, ROWS), dst_ref=rows_of(field.at[A], lo, n, TOP, ROWS),
            send_sem=shift_sem.at[k], recv_sem=arrive_sem.at[k],
            device_id=(g + 1, r), device_id_type=MESH,
        )

    def inner(which, k, depth):
        lo, n = chunk(k)
        f = field.at[which]
        return [
            (core == 1 - side, sides(f, f, lo, n, depth, halo_send.at[which, 0, k], halo_recv.at[which, 0, k], g, sibling, side))
            for side in (0, 1)
        ]

    def outside(which, k, depth):
        lo, n = chunk(k)
        f = field.at[which]
        return [
            (core == side, sides(f, f, lo, n, depth, halo_send.at[which, 1, k], halo_recv.at[which, 1, k], g, outer, side))
            for side in (0, 1)
        ]

    def onward(k, depth):
        lo, n = chunk(k)
        return [
            (core == side, sides(field.at[B], field.at[A], lo, n, depth, edge_sem.at[k], arrive_sem.at[k], g + 1, outer, side))
            for side in (0, 1)
        ]

    def back(k):
        lo, n = chunk(k)
        return [
            (core == side, sides(spare, field.at[A], lo, n, DEEP, edge_sem.at[n_windows + k], arrive_sem.at[k], 0, outer, side))
            for side in (0, 1)
        ]

    def each(copies, method):
        for condition, copy in copies:
            pl.when(condition)(getattr(copy, method))

    def got(which, side, k, depth):
        lo, n = chunk(k)
        await_bytes(rows_of(field.at[which], lo, n, TOP, depth), halo_recv.at[which, side, k])

    @pl.when(g == 1)
    def _():
        for k in range(n_windows):
            lo, n = chunk(k)
            await_bytes(rows_of(spare, lo, n, TOP, ROWS), load_sem.at[1, k])
            each(back(k), "start")

    for k in range(n_windows):
        lo, n = chunk(k)
        await_bytes(rows_of(field.at[B], lo, n, TOP, ROWS), load_sem.at[0, k])

        @pl.when(has_far)
        def _(k=k):
            each(outside(B, k, OWN), "start")
            each(inner(B, k, OWN), "start")

        @pl.when(has_next & even)
        def _(k=k):
            each(onward(k, SHALLOW), "start")
            shift(k).start()

        @pl.when(has_next & ~even)
        def _(k=k):
            each(onward(k, DEEP), "start")
            shift(k).start()

    def arrived(k):
        lo, n = chunk(k)

        @pl.when(even)
        def _():
            await_bytes(rows_of(field.at[A], lo, n, TOP, ROWS + DEEP), arrive_sem.at[k])
            each(inner(A, k, DEEP), "start")

        @pl.when(~even)
        def _():
            await_bytes(rows_of(field.at[A], lo, n, TOP, ROWS + SHALLOW), arrive_sem.at[k])
            each(inner(A, k, SHALLOW), "start")

    def wrap(ref, lo, to, n):
        for i in range(n):
            ref[to + i] = ref[lo + i]

    def fine(src, dst, base, wide, row, rows):
        def one(i, _):
            dst[base + i, :, pl.ds(row, rows), :] = update(src, base, i, wide + 2, row, rows, FINE)
            return 0

        lax.fori_loop(1, wide + 2, one, 0, unroll=True)

    def excess(w, out, base, wide, row, rows, rough):
        def one(i, _):
            t = update(w.at[6], base, i, wide + 2, row, rows, FINE)
            if rough:
                t = t - update(w.at[STEPS - 1], base, i, wide + 2, row, rows, COARSE)
            out[base + i, :, pl.ds(row, rows), :] = t
            return 0

        lax.fori_loop(1, wide + 2, one, 0, unroll=True)

    def mend(ref, row, rows):
        lane = lax.broadcasted_iota(jnp.int32, (2, rows, LANES), 2)
        here = pl.ds(row, rows)
        ref[1, :, here, :] = jnp.where(lane < LANES // 2, ref[cols + 1, :, here, :], ref[1, :, here, :])

    def march_own(k):
        for q in range(cols // BROAD):
            @pl.when(k == q)
            def _(q=q):
                for p in range(q * BROAD // WIDE, (q + 1) * BROAD // WIDE):
                    got(B, 0, p, OWN)
                    got(B, 1, p, OWN)
                if q == cols // BROAD - 1:
                    wrap(field.at[B], 0, cols, 2)

        w = steps.at[B]
        base = BROAD * k
        fine(field.at[B], w.at[0], base, BROAD, TOP - 8, 48)
        for n in range(1, 7):
            row, rows = (TOP - 8, 48) if n < 3 else (TOP - 4, 40)
            fine(w.at[n - 1], w.at[n], base, BROAD, row, rows)
        excess(w, tau.at[B], base, BROAD, TOP, ROWS, True)

    def put(f):
        there = pl.ds(pl.multiple_of((f - 1) * LANES, LANES), LANES)
        relaxed[f, :, strip, :] = steps[A, STEPS - 1, f, :, strip, :]
        pltpu.make_async_copy(relaxed.at[f, :, strip, :], relaxed_ref.at[:, :, there], out_sem.at[0]).start()

        @pl.when(g == 0)
        def _():
            pltpu.make_async_copy(relaxed.at[f, :, strip, :], corrected_ref.at[:, :, there], out_sem.at[1]).start()

    def march_prior(k):
        for q in range(n_windows):
            @pl.when(k == q)
            def _(q=q):
                @pl.when(even)
                def _():
                    got(A, 0, q, DEEP)

                @pl.when(~even)
                def _():
                    got(A, 0, q, SHALLOW)

                if q == n_windows - 1:
                    wrap(field.at[A], 0, cols, 2)

        base = WIDE * k
        w = steps.at[A]
        row, rows = TOP - 4, 40
        fine(field.at[A], w.at[0], base, WIDE, TOP - 8, 48)
        for n in range(1, STEPS):
            fine(w.at[n - 1], w.at[n], base, WIDE, TOP - 8, 48)

        def one(f, _):
            put(f)
            return 0

        lax.fori_loop(jnp.maximum(base + 1, 2), base + WIDE + 1, one, 0)

        @pl.when(k == n_windows - 1)
        def _():
            mend(steps.at[A, STEPS - 1], TOP, ROWS)
            put(1)

        @pl.when(even)
        def _():
            for n in range(STEPS, 7):
                fine(w.at[n - 1], w.at[n], base, WIDE, row, rows)

            @pl.when(g == 0)
            def _():
                excess(w, tau.at[A], base, WIDE, row, rows, False)

            @pl.when(g > 0)
            def _():
                excess(w, tau.at[A], base, WIDE, row, rows, True)

    def put_out(ref, p, offset):
        c = lax.rem(p + offset, cols)
        pltpu.make_async_copy(
            ref.at[p, :, strip, :],
            corrected_ref.at[:, :, pl.ds(pl.multiple_of(c * LANES, LANES), LANES)],
            out_sem.at[1],
        ).start()

    def group_in(j, extra):
        await_bytes(rows_of(state, GROUP * j, GROUP, TOP - extra, ROWS + 2 * extra), chain_recv.at[j])

    def group_out(j):
        def copy(row_from, n, row_to, device):
            return pltpu.make_async_remote_copy(
                src_ref=rows_of(nxt, GROUP * j, GROUP, row_from, n),
                dst_ref=rows_of(state, GROUP * j, GROUP, row_to, n),
                send_sem=chain_send.at[j], recv_sem=chain_recv.at[j],
                device_id=(g + 2, device), device_id_type=MESH,
            )

        copy(TOP, EDGE, TOP + ROWS, down).start()
        copy(TOP + ROWS - EDGE, EDGE, TOP - EDGE, up).start()
        copy(TOP, ROWS, TOP, r).start()

    def pass_on(j, src, first):
        return pltpu.make_async_remote_copy(
            src_ref=rows_of(src, first, GROUP, TOP, ROWS),
            dst_ref=rows_of(state, GROUP * j, GROUP, TOP, ROWS),
            send_sem=pass_send.at[j], recv_sem=chain_recv.at[j],
            device_id=(g + 1, r), device_id_type=MESH,
        )

    def chain(j, _):
        base = GROUP * j
        row, rows = TOP - 4, 40

        def onward_state(src, first):
            def rough(i, _):
                nxt[base + i, :, strip, :] = update(src, first, i + 1, GROUP + 2, TOP, ROWS, COARSE) + tau[B, base + x + 2 + i, :, strip, :]
                return 0

            lax.fori_loop(0, GROUP, rough, 0, unroll=True)
            group_out(j)

        @pl.when(x > 0)
        def _():
            @pl.when(j == 0)
            def _():
                group_in(0, EDGE)
                wrap(state, 0, cols, 2)
                for i in range(GROUP):
                    put_out(state, i, x)

            @pl.when(j < n_groups - 1)
            def _():
                group_in(j + 1, EDGE)
                for i in range(GROUP):
                    put_out(state, GROUP * (j + 1) + i, x)

            def rough(i, _):
                mid[i, :, pl.ds(row, rows), :] = update(state, base, i, GROUP + 2, row, rows, COARSE) + tau[A, base + x + 1 + i, :, pl.ds(row, rows), :]
                return 0

            lax.fori_loop(0, GROUP + 2, rough, 0, unroll=True)

            @pl.when(has_far)
            def _():
                onward_state(mid, 0)

            for i in range(GROUP):
                odd_state[base + i, :, strip, :] = mid[1 + i, :, strip, :]
            pass_on(j, odd_state, base).start()

        @pl.when(x == 0)
        def _():
            onward_state(tau.at[A], base + 1)
            pass_on(j, tau.at[A], base + 2).start()

        return 0

    ahead = WIDE // GROUP
    lead = jnp.where(x == 0, 0, 1)
    per = BROAD // WIDE

    def rounds(k, _):
        now = (k >= 0) & (k < n_windows)
        for q in range(n_windows):
            @pl.when((k == q) & ((x == 0) | (q == 0)))
            def _(q=q):
                arrived(q)

        @pl.when(has_far & (k + lead < n_windows) & (lax.rem(k + lead, per) == 0))
        def _():
            march_own((k + lead) // per)

        @pl.when(now)
        def _():
            march_prior(k)

        for q in range(n_windows - 1):
            @pl.when((x > 0) & (k == q))
            def _(q=q):
                arrived(q + 1)

        @pl.when(has_far & (k == n_windows))
        def _():
            mend(tau.at[B], TOP, ROWS)
            tau[B, cols + 1] = tau[B, 1]
            for i in range(1, 5):
                tau[B, cols + 1 + i] = tau[B, 1 + i]

        @pl.when(even & (k == n_windows))
        def _():
            mend(tau.at[A], TOP - 4, 40)
            for i in range(5):
                tau[A, cols + 1 + i] = tau[A, 1 + i]

        @pl.when(even)
        def _():
            first = jnp.maximum(ahead * (k - 1) + 1 - x, 0)
            stop = jnp.maximum(ahead * k + 1 - x, 0)
            lax.fori_loop(first, jnp.where(k == n_windows, n_groups, stop), chain, 0)

        return 0

    lax.fori_loop(-lead, n_windows + 1, rounds, 0)

    @pl.when(~even)
    def _():
        def one(j, _):
            group_in(j, 0)
            for i in range(GROUP):
                put_out(state, GROUP * j + i, x + 1)
            return 0

        lax.fori_loop(0, n_groups, one, 0)

    for k in range(n_windows):
        @pl.when(has_far)
        def _(k=k):
            each(outside(B, k, OWN), "wait_send")
            each(inner(B, k, OWN), "wait_send")

        @pl.when(has_next & even)
        def _(k=k):
            each(onward(k, SHALLOW), "wait_send")

        @pl.when(has_next & ~even)
        def _(k=k):
            each(onward(k, DEEP), "wait_send")

        @pl.when(has_next)
        def _(k=k):
            shift(k).wait_send()

        @pl.when(even)
        def _(k=k):
            each(inner(A, k, DEEP), "wait_send")

        @pl.when(~even)
        def _(k=k):
            each(inner(A, k, SHALLOW), "wait_send")

        @pl.when(g == 1)
        def _(k=k):
            each(back(k), "wait_send")

    @pl.when(even)
    def _():
        def one(j, _):
            pass_on(j, odd_state, 0).wait_send()

            @pl.when(has_far)
            def _():
                await_bytes(rows_of(nxt, GROUP * j, GROUP, TOP, ROWS + 2 * EDGE), chain_send.at[j])

            return 0

        lax.fori_loop(0, n_groups, one, 0)

    for i in range(2):
        await_bytes(rows_of(relaxed, 1, cols, TOP, ROWS), out_sem.at[i])


def shards(start_state, guess):
    guess = guess[0]
    width = guess.shape[2]
    cols = width // LANES
    strips = lax.axis_size("rows")
    groups = lax.axis_size("tm")
    out = jax.ShapeDtypeStruct(guess.shape, guess.dtype)
    n_windows = cols // WIDE
    n_groups = cols // GROUP

    def frames(*lead):
        return pltpu.VMEM((*lead, 2, FRAME, LANES), jnp.float32)

    dma = pltpu.SemaphoreType.DMA
    corrected, relaxed = pl.pallas_call(
        functools.partial(kernel, cols, groups, strips),
        out_shape=(out, out),
        in_specs=[pl.BlockSpec(memory_space=pltpu.HBM)] * 2,
        out_specs=(pl.BlockSpec(memory_space=pl.ANY),) * 2,
        scratch_shapes=[
            frames(2, cols + 2), frames(cols), frames(2, cols + 6), frames(2, 7, cols + 2),
            frames(cols + 1), frames(cols + 2), frames(GROUP + 2), frames(cols), frames(cols),
            dma((2, n_windows)), dma((n_windows,)), dma((n_windows,)), dma((2 * n_windows,)),
            dma((2, 2, n_windows)), dma((2, 2, n_windows)),
            dma((n_groups,)), dma((n_groups,)), dma((n_groups,)), dma((2,)),
        ],
        compiler_params=pltpu.CompilerParams(
            collective_id=0, has_side_effects=True, vmem_limit_bytes=51 * 2**20
        ),
    )(start_state, guess)
    return corrected[None], relaxed[None]


def solution(mesh):
    return jax.shard_map(
        shards,
        mesh=mesh,
        in_specs=(P(None, "rows", None), P("tm", None, "rows", None)),
        out_specs=(P("tm", None, "rows", None), P("tm", None, "rows", None)),
        check_vma=False,
    )
```

```python
import functools

import jax
import jax.numpy as jnp
from jax import lax
from jax.experimental import pallas as pl
from jax.experimental.pallas import tpu as pltpu
from jax.sharding import PartitionSpec as P

STEPS = 4
FINE = 0.05
COARSE = STEPS * FINE
VISCOSITY = 1.0
MESH = pl.DeviceIdType.MESH

LANES = 128
TOP = 16
FRAME = 64
ROWS = 32
DEEP = 9
OWN = 8
SHALLOW = 4
EDGE = 2
WIDE = 4
SPAN = WIDE + 2
BROAD = 4
GROUP = 2


def update(src, base, i, count, row, rows, size):
    lane = lax.broadcasted_iota(jnp.int32, (2, rows, LANES), 2)
    here = pl.ds(row, rows)
    left = base + jnp.maximum(i - 1, 0)
    right = base + jnp.minimum(i + 1, count - 1)
    c = src[base + i, :, here, :]
    east = pltpu.roll(jnp.where(lane == 0, src[right, :, here, :], c), LANES - 1, 2)
    west = pltpu.roll(jnp.where(lane == LANES - 1, src[left, :, here, :], c), 1, 2)
    upper = src[base + i, :, pl.ds(row + 1, rows), :]
    lower = src[base + i, :, pl.ds(row - 1, rows), :]
    u = (0.5 * size) * c[0:1]
    v = (0.5 * size) * c[1:2]
    k = size * VISCOSITY
    return (1.0 - 4.0 * k) * c + ((k - u) * east + (k + u) * west) + ((k - v) * upper + (k + v) * lower)


def kernel(
    cols, groups, strips, start_ref, guess_ref, corrected_ref, relaxed_ref,
    field, spare, tau, steps, relaxed, state, mid, odd_state, nxt,
    load_sem, arrive_sem, shift_sem, edge_sem, halo_send, halo_recv,
    chain_send, chain_recv, pass_send, out_sem,
):
    g = lax.axis_index("tm")
    r = lax.axis_index("rows")
    x = g // 2
    even = lax.rem(g, 2) == 0
    core = lax.rem(r, 2)
    up = lax.rem(r + 1, strips)
    down = lax.rem(r + strips - 1, strips)
    sibling = r + 1 - 2 * core
    outer = jnp.where(core == 0, down, up)
    n_windows = cols // WIDE
    n_groups = cols // GROUP
    strip = pl.ds(TOP, ROWS)
    B, A = 0, 1
    has_next = g < groups - 1
    has_far = even & (g < groups - 2)

    barrier = pltpu.get_barrier_semaphore()

    def greet(group, row):
        pl.semaphore_signal(barrier, inc=1, device_id=(group, row), device_id_type=MESH)

    greet(g, up)
    greet(g, down)

    @pl.when(g == 0)
    def _():
        greet(1, outer)

    @pl.when(g >= 1)
    def _():
        greet(g - 1, r)
        greet(g - 1, outer)

    @pl.when(even & (g >= 2))
    def _():
        greet(g - 2, r)
        greet(g - 2, up)
        greet(g - 2, down)

    def chunk(k):
        if k == 0:
            return 0, SPAN
        if k < n_windows - 1:
            return WIDE * k + 2, WIDE
        return WIDE * k + 2, WIDE - 2

    def load(src, dst, sems):
        for k in range(n_windows):
            lo, n = chunk(k)

            def one(f, _, k=k):
                c = lax.rem(f + cols - 1, cols)
                pltpu.make_async_copy(
                    src.at[:, :, pl.ds(pl.multiple_of(c * LANES, LANES), LANES)],
                    dst.at[f, :, strip, :],
                    sems.at[k],
                ).start()
                return 0

            lax.fori_loop(lo, lo + n, one, 0)

    load(guess_ref, field.at[B], load_sem.at[0])

    @pl.when(g == 0)
    def _():
        load(start_ref, field.at[A], arrive_sem)

    @pl.when(g == 1)
    def _():
        load(start_ref, spare, load_sem.at[1])

    pl.semaphore_wait(
        barrier,
        2 + jnp.where(has_next, 2, 0) + jnp.where(g == 1, 1, 0) + jnp.where(has_far, 3, 0),
    )

    def rows_of(ref, lo, n, row, count):
        return ref.at[pl.ds(lo, n), :, pl.ds(row, count), :]

    def await_bytes(ref, sem):
        pltpu.make_async_copy(ref, ref, sem).wait()

    def sides(src, dst, lo, n, depth, send, recv, group, device, side):
        row_from, row_to = ((TOP, TOP + ROWS), (TOP + ROWS - depth, TOP - depth))[side]
        return pltpu.make_async_remote_copy(
            src_ref=rows_of(src, lo, n, row_from, depth), dst_ref=rows_of(dst, lo, n, row_to, depth),
            send_sem=send, recv_sem=recv, device_id=(group, device), device_id_type=MESH,
        )

    def shift(k):
        lo, n = chunk(k)
        return pltpu.make_async_remote_copy(
            src_ref=rows_of(field.at[B], lo, n, TOP, ROWS), dst_ref=rows_of(field.at[A], lo, n, TOP, ROWS),
            send_sem=shift_sem.at[k], recv_sem=arrive_sem.at[k],
            device_id=(g + 1, r), device_id_type=MESH,
        )

    def inner(which, k, depth):
        lo, n = chunk(k)
        f = field.at[which]
        return [
            (core == 1 - side, sides(f, f, lo, n, depth, halo_send.at[which, 0, k], halo_recv.at[which, 0, k], g, sibling, side))
            for side in (0, 1)
        ]

    def outside(which, k, depth):
        lo, n = chunk(k)
        f = field.at[which]
        return [
            (core == side, sides(f, f, lo, n, depth, halo_send.at[which, 1, k], halo_recv.at[which, 1, k], g, outer, side))
            for side in (0, 1)
        ]

    def onward(k, depth):
        lo, n = chunk(k)
        return [
            (core == side, sides(field.at[B], field.at[A], lo, n, depth, edge_sem.at[k], arrive_sem.at[k], g + 1, outer, side))
            for side in (0, 1)
        ]

    def back(k):
        lo, n = chunk(k)
        return [
            (core == side, sides(spare, field.at[A], lo, n, DEEP, edge_sem.at[n_windows + k], arrive_sem.at[k], 0, outer, side))
            for side in (0, 1)
        ]

    def each(copies, method):
        for condition, copy in copies:
            pl.when(condition)(getattr(copy, method))

    def got(which, side, k, depth):
        lo, n = chunk(k)
        await_bytes(rows_of(field.at[which], lo, n, TOP, depth), halo_recv.at[which, side, k])

    @pl.when(g == 1)
    def _():
        for k in range(n_windows):
            lo, n = chunk(k)
            await_bytes(rows_of(spare, lo, n, TOP, ROWS), load_sem.at[1, k])
            each(back(k), "start")

    for k in range(n_windows):
        lo, n = chunk(k)
        await_bytes(rows_of(field.at[B], lo, n, TOP, ROWS), load_sem.at[0, k])

        @pl.when(has_far)
        def _(k=k):
            each(outside(B, k, OWN), "start")
            each(inner(B, k, OWN), "start")

        @pl.when(has_next & even)
        def _(k=k):
            each(onward(k, SHALLOW), "start")
            shift(k).start()

        @pl.when(has_next & ~even)
        def _(k=k):
            each(onward(k, DEEP), "start")
            shift(k).start()

    def arrived(k):
        lo, n = chunk(k)

        @pl.when(even)
        def _():
            await_bytes(rows_of(field.at[A], lo, n, TOP, ROWS + DEEP), arrive_sem.at[k])
            each(inner(A, k, DEEP), "start")

        @pl.when(~even)
        def _():
            await_bytes(rows_of(field.at[A], lo, n, TOP, ROWS + SHALLOW), arrive_sem.at[k])
            each(inner(A, k, SHALLOW), "start")

    def wrap(ref, lo, to, n):
        for i in range(n):
            ref[to + i] = ref[lo + i]

    def fine(src, dst, base, wide, row, rows):
        def one(i, _):
            dst[base + i, :, pl.ds(row, rows), :] = update(src, base, i, wide + 2, row, rows, FINE)
            return 0

        lax.fori_loop(1, wide + 2, one, 0, unroll=True)

    def excess(w, out, base, wide, row, rows, rough):
        def one(i, _):
            t = update(w.at[6], base, i, wide + 2, row, rows, FINE)
            if rough:
                t = t - update(w.at[STEPS - 1], base, i, wide + 2, row, rows, COARSE)
            out[base + i, :, pl.ds(row, rows), :] = t
            return 0

        lax.fori_loop(1, wide + 2, one, 0, unroll=True)

    def mend(ref, row, rows):
        lane = lax.broadcasted_iota(jnp.int32, (2, rows, LANES), 2)
        here = pl.ds(row, rows)
        ref[1, :, here, :] = jnp.where(lane < LANES // 2, ref[cols + 1, :, here, :], ref[1, :, here, :])

    def march_own(k):
        for q in range(cols // BROAD):
            @pl.when(k == q)
            def _(q=q):
                for p in range(q * BROAD // WIDE, (q + 1) * BROAD // WIDE):
                    got(B, 0, p, OWN)
                    got(B, 1, p, OWN)
                if q == cols // BROAD - 1:
                    wrap(field.at[B], 0, cols, 2)

        w = steps.at[B]
        base = BROAD * k
        fine(field.at[B], w.at[0], base, BROAD, TOP - 8, 48)
        for n in range(1, 7):
            row, rows = (TOP - 8, 48) if n < 3 else (TOP - 4, 40)
            fine(w.at[n - 1], w.at[n], base, BROAD, row, rows)
        excess(w, tau.at[B], base, BROAD, TOP, ROWS, True)

    def put(f):
        there = pl.ds(pl.multiple_of((f - 1) * LANES, LANES), LANES)
        relaxed[f, :, strip, :] = steps[A, STEPS - 1, f, :, strip, :]
        pltpu.make_async_copy(relaxed.at[f, :, strip, :], relaxed_ref.at[:, :, there], out_sem.at[0]).start()

        @pl.when(g == 0)
        def _():
            pltpu.make_async_copy(relaxed.at[f, :, strip, :], corrected_ref.at[:, :, there], out_sem.at[1]).start()

    def march_prior(k):
        for q in range(n_windows):
            @pl.when(k == q)
            def _(q=q):
                @pl.when(even)
                def _():
                    got(A, 0, q, DEEP)

                @pl.when(~even)
                def _():
                    got(A, 0, q, SHALLOW)

                if q == n_windows - 1:
                    wrap(field.at[A], 0, cols, 2)

        base = WIDE * k
        w = steps.at[A]
        row, rows = TOP - 4, 40
        fine(field.at[A], w.at[0], base, WIDE, TOP - 8, 48)
        for n in range(1, STEPS):
            fine(w.at[n - 1], w.at[n], base, WIDE, TOP - 8, 48)

        def one(f, _):
            put(f)
            return 0

        lax.fori_loop(jnp.maximum(base + 1, 2), base + WIDE + 1, one, 0)

        @pl.when(k == n_windows - 1)
        def _():
            mend(steps.at[A, STEPS - 1], TOP, ROWS)
            put(1)

        @pl.when(even)
        def _():
            for n in range(STEPS, 7):
                fine(w.at[n - 1], w.at[n], base, WIDE, row, rows)

            @pl.when(g == 0)
            def _():
                excess(w, tau.at[A], base, WIDE, row, rows, False)

            @pl.when(g > 0)
            def _():
                excess(w, tau.at[A], base, WIDE, row, rows, True)

    def put_out(ref, p, offset):
        c = lax.rem(p + offset, cols)
        pltpu.make_async_copy(
            ref.at[p, :, strip, :],
            corrected_ref.at[:, :, pl.ds(pl.multiple_of(c * LANES, LANES), LANES)],
            out_sem.at[1],
        ).start()

    def group_in(j, extra):
        await_bytes(rows_of(state, GROUP * j, GROUP, TOP - extra, ROWS + 2 * extra), chain_recv.at[j])

    def group_out(j):
        def copy(row_from, n, row_to, device):
            return pltpu.make_async_remote_copy(
                src_ref=rows_of(nxt, GROUP * j, GROUP, row_from, n),
                dst_ref=rows_of(state, GROUP * j, GROUP, row_to, n),
                send_sem=chain_send.at[j], recv_sem=chain_recv.at[j],
                device_id=(g + 2, device), device_id_type=MESH,
            )

        copy(TOP, EDGE, TOP + ROWS, down).start()
        copy(TOP + ROWS - EDGE, EDGE, TOP - EDGE, up).start()
        copy(TOP, ROWS, TOP, r).start()

    def pass_on(j, src, first):
        return pltpu.make_async_remote_copy(
            src_ref=rows_of(src, first, GROUP, TOP, ROWS),
            dst_ref=rows_of(state, GROUP * j, GROUP, TOP, ROWS),
            send_sem=pass_send.at[j], recv_sem=chain_recv.at[j],
            device_id=(g + 1, r), device_id_type=MESH,
        )

    def chain(j, _):
        base = GROUP * j
        row, rows = TOP - 4, 40

        def onward_state(src, first):
            def rough(i, _):
                nxt[base + i, :, strip, :] = update(src, first, i + 1, GROUP + 2, TOP, ROWS, COARSE) + tau[B, base + x + 2 + i, :, strip, :]
                return 0

            lax.fori_loop(0, GROUP, rough, 0, unroll=True)
            group_out(j)

        @pl.when(x > 0)
        def _():
            @pl.when(j == 0)
            def _():
                group_in(0, EDGE)
                wrap(state, 0, cols, 2)
                for i in range(GROUP):
                    put_out(state, i, x)

            @pl.when(j < n_groups - 1)
            def _():
                group_in(j + 1, EDGE)
                for i in range(GROUP):
                    put_out(state, GROUP * (j + 1) + i, x)

            def rough(i, _):
                mid[i, :, pl.ds(row, rows), :] = update(state, base, i, GROUP + 2, row, rows, COARSE) + tau[A, base + x + 1 + i, :, pl.ds(row, rows), :]
                return 0

            lax.fori_loop(0, GROUP + 2, rough, 0, unroll=True)

            @pl.when(has_far)
            def _():
                onward_state(mid, 0)

            for i in range(GROUP):
                odd_state[base + i, :, strip, :] = mid[1 + i, :, strip, :]
            pass_on(j, odd_state, base).start()

        @pl.when(x == 0)
        def _():
            onward_state(tau.at[A], base + 1)
            pass_on(j, tau.at[A], base + 2).start()

        return 0

    ahead = WIDE // GROUP
    lead = jnp.where(x == 0, 0, 1)
    per = BROAD // WIDE

    def rounds(k, _):
        now = (k >= 0) & (k < n_windows)
        for q in range(n_windows):
            @pl.when((k == q) & ((x == 0) | (q == 0)))
            def _(q=q):
                arrived(q)

        @pl.when(has_far & (k + lead < n_windows) & (lax.rem(k + lead, per) == 0))
        def _():
            march_own((k + lead) // per)

        @pl.when(now)
        def _():
            march_prior(k)

        for q in range(n_windows - 1):
            @pl.when((x > 0) & (k == q))
            def _(q=q):
                arrived(q + 1)

        @pl.when(has_far & (k == n_windows))
        def _():
            mend(tau.at[B], TOP, ROWS)
            tau[B, cols + 1] = tau[B, 1]
            for i in range(1, 5):
                tau[B, cols + 1 + i] = tau[B, 1 + i]

        @pl.when(even & (k == n_windows))
        def _():
            mend(tau.at[A], TOP - 4, 40)
            for i in range(5):
                tau[A, cols + 1 + i] = tau[A, 1 + i]

        @pl.when(even)
        def _():
            lag = jnp.maximum(x - 1, 0)
            first = jnp.maximum(ahead * (k - 1) + 1 - lag, 0)
            stop = jnp.maximum(ahead * k + 1 - lag, 0)
            lax.fori_loop(first, jnp.where(k == n_windows, n_groups, stop), chain, 0)

        return 0

    lax.fori_loop(-lead, n_windows + 1, rounds, 0)

    @pl.when(~even)
    def _():
        def one(j, _):
            group_in(j, 0)
            for i in range(GROUP):
                put_out(state, GROUP * j + i, x + 1)
            return 0

        lax.fori_loop(0, n_groups, one, 0)

    for k in range(n_windows):
        @pl.when(has_far)
        def _(k=k):
            each(outside(B, k, OWN), "wait_send")
            each(inner(B, k, OWN), "wait_send")

        @pl.when(has_next & even)
        def _(k=k):
            each(onward(k, SHALLOW), "wait_send")

        @pl.when(has_next & ~even)
        def _(k=k):
            each(onward(k, DEEP), "wait_send")

        @pl.when(has_next)
        def _(k=k):
            shift(k).wait_send()

        @pl.when(even)
        def _(k=k):
            each(inner(A, k, DEEP), "wait_send")

        @pl.when(~even)
        def _(k=k):
            each(inner(A, k, SHALLOW), "wait_send")

        @pl.when(g == 1)
        def _(k=k):
            each(back(k), "wait_send")

    @pl.when(even)
    def _():
        def one(j, _):
            pass_on(j, odd_state, 0).wait_send()

            @pl.when(has_far)
            def _():
                await_bytes(rows_of(nxt, GROUP * j, GROUP, TOP, ROWS + 2 * EDGE), chain_send.at[j])

            return 0

        lax.fori_loop(0, n_groups, one, 0)

    for i in range(2):
        await_bytes(rows_of(relaxed, 1, cols, TOP, ROWS), out_sem.at[i])


def shards(start_state, guess):
    guess = guess[0]
    width = guess.shape[2]
    cols = width // LANES
    strips = lax.axis_size("rows")
    groups = lax.axis_size("tm")
    out = jax.ShapeDtypeStruct(guess.shape, guess.dtype)
    n_windows = cols // WIDE
    n_groups = cols // GROUP

    def frames(*lead):
        return pltpu.VMEM((*lead, 2, FRAME, LANES), jnp.float32)

    dma = pltpu.SemaphoreType.DMA
    corrected, relaxed = pl.pallas_call(
        functools.partial(kernel, cols, groups, strips),
        out_shape=(out, out),
        in_specs=[pl.BlockSpec(memory_space=pltpu.HBM)] * 2,
        out_specs=(pl.BlockSpec(memory_space=pl.ANY),) * 2,
        scratch_shapes=[
            frames(2, cols + 2), frames(cols), frames(2, cols + 6), frames(2, 7, cols + 2),
            frames(cols + 1), frames(cols + 2), frames(GROUP + 2), frames(cols), frames(cols),
            dma((2, n_windows)), dma((n_windows,)), dma((n_windows,)), dma((2 * n_windows,)),
            dma((2, 2, n_windows)), dma((2, 2, n_windows)),
            dma((n_groups,)), dma((n_groups,)), dma((n_groups,)), dma((2,)),
        ],
        compiler_params=pltpu.CompilerParams(
            collective_id=0, has_side_effects=True, vmem_limit_bytes=51 * 2**20
        ),
    )(start_state, guess)
    return corrected[None], relaxed[None]


def solution(mesh):
    return jax.shard_map(
        shards,
        mesh=mesh,
        in_specs=(P(None, "rows", None), P("tm", None, "rows", None)),
        out_specs=(P("tm", None, "rows", None), P("tm", None, "rows", None)),
        check_vma=False,
    )
```

```python
import functools

import jax
import jax.numpy as jnp
from jax import lax
from jax.experimental import pallas as pl
from jax.experimental.pallas import tpu as pltpu
from jax.sharding import PartitionSpec as P

STEPS = 4
FINE = 0.05
COARSE = STEPS * FINE
VISCOSITY = 1.0
MESH = pl.DeviceIdType.MESH

LANES = 128
TOP = 16
FRAME = 64
ROWS = 32
DEEP = 9
OWN = 8
SHALLOW = 4
EDGE = 2
WIDE = 4
SPAN = WIDE + 2
BROAD = 4
GROUP = 2


def update(src, base, i, count, row, rows, size):
    lane = lax.broadcasted_iota(jnp.int32, (2, rows, LANES), 2)
    here = pl.ds(row, rows)
    left = base + jnp.maximum(i - 1, 0)
    right = base + jnp.minimum(i + 1, count - 1)
    c = src[base + i, :, here, :]
    east = pltpu.roll(jnp.where(lane == 0, src[right, :, here, :], c), LANES - 1, 2)
    west = pltpu.roll(jnp.where(lane == LANES - 1, src[left, :, here, :], c), 1, 2)
    upper = src[base + i, :, pl.ds(row + 1, rows), :]
    lower = src[base + i, :, pl.ds(row - 1, rows), :]
    u = (0.5 * size) * c[0:1]
    v = (0.5 * size) * c[1:2]
    k = size * VISCOSITY
    return (1.0 - 4.0 * k) * c + ((k - u) * east + (k + u) * west) + ((k - v) * upper + (k + v) * lower)


def kernel(
    cols, groups, strips, start_ref, guess_ref, corrected_ref, relaxed_ref,
    field, spare, tau, steps, relaxed, state, mid, odd_state, nxt,
    load_sem, arrive_sem, shift_sem, edge_sem, halo_send, halo_recv,
    chain_send, chain_recv, pass_send, out_sem,
):
    g = lax.axis_index("tm")
    r = lax.axis_index("rows")
    x = g // 2
    even = lax.rem(g, 2) == 0
    core = lax.rem(r, 2)
    up = lax.rem(r + 1, strips)
    down = lax.rem(r + strips - 1, strips)
    sibling = r + 1 - 2 * core
    outer = jnp.where(core == 0, down, up)
    n_windows = cols // WIDE
    n_groups = cols // GROUP
    strip = pl.ds(TOP, ROWS)
    B, A = 0, 1
    has_next = g < groups - 1
    has_far = even & (g < groups - 2)

    barrier = pltpu.get_barrier_semaphore()

    def greet(group, row):
        pl.semaphore_signal(barrier, inc=1, device_id=(group, row), device_id_type=MESH)

    greet(g, up)
    greet(g, down)

    @pl.when(g == 0)
    def _():
        greet(1, outer)

    @pl.when(g >= 1)
    def _():
        greet(g - 1, r)
        greet(g - 1, outer)

    @pl.when(even & (g >= 2))
    def _():
        greet(g - 2, r)
        greet(g - 2, up)
        greet(g - 2, down)

    def chunk(k):
        if k == 0:
            return 0, SPAN
        if k < n_windows - 1:
            return WIDE * k + 2, WIDE
        return WIDE * k + 2, WIDE - 2

    def load(src, dst, sems):
        for k in range(n_windows):
            lo, n = chunk(k)

            def one(f, _, k=k):
                c = lax.rem(f + cols - 1, cols)
                pltpu.make_async_copy(
                    src.at[:, :, pl.ds(pl.multiple_of(c * LANES, LANES), LANES)],
                    dst.at[f, :, strip, :],
                    sems.at[k],
                ).start()
                return 0

            lax.fori_loop(lo, lo + n, one, 0)

    load(guess_ref, field.at[B], load_sem.at[0])

    @pl.when(g == 0)
    def _():
        load(start_ref, field.at[A], arrive_sem)

    @pl.when(g == 1)
    def _():
        load(start_ref, spare, load_sem.at[1])

    pl.semaphore_wait(
        barrier,
        2 + jnp.where(has_next, 2, 0) + jnp.where(g == 1, 1, 0) + jnp.where(has_far, 3, 0),
    )

    def rows_of(ref, lo, n, row, count):
        return ref.at[pl.ds(lo, n), :, pl.ds(row, count), :]

    def await_bytes(ref, sem):
        pltpu.make_async_copy(ref, ref, sem).wait()

    def sides(src, dst, lo, n, depth, send, recv, group, device, side):
        row_from, row_to = ((TOP, TOP + ROWS), (TOP + ROWS - depth, TOP - depth))[side]
        return pltpu.make_async_remote_copy(
            src_ref=rows_of(src, lo, n, row_from, depth), dst_ref=rows_of(dst, lo, n, row_to, depth),
            send_sem=send, recv_sem=recv, device_id=(group, device), device_id_type=MESH,
        )

    def shift(k):
        lo, n = chunk(k)
        return pltpu.make_async_remote_copy(
            src_ref=rows_of(field.at[B], lo, n, TOP, ROWS), dst_ref=rows_of(field.at[A], lo, n, TOP, ROWS),
            send_sem=shift_sem.at[k], recv_sem=arrive_sem.at[k],
            device_id=(g + 1, r), device_id_type=MESH,
        )

    def inner(which, k, depth):
        lo, n = chunk(k)
        f = field.at[which]
        return [
            (core == 1 - side, sides(f, f, lo, n, depth, halo_send.at[which, 0, k], halo_recv.at[which, 0, k], g, sibling, side))
            for side in (0, 1)
        ]

    def outside(which, k, depth):
        lo, n = chunk(k)
        f = field.at[which]
        return [
            (core == side, sides(f, f, lo, n, depth, halo_send.at[which, 1, k], halo_recv.at[which, 1, k], g, outer, side))
            for side in (0, 1)
        ]

    def onward(k, depth):
        lo, n = chunk(k)
        return [
            (core == side, sides(field.at[B], field.at[A], lo, n, depth, edge_sem.at[k], arrive_sem.at[k], g + 1, outer, side))
            for side in (0, 1)
        ]

    def back(k):
        lo, n = chunk(k)
        return [
            (core == side, sides(spare, field.at[A], lo, n, DEEP, edge_sem.at[n_windows + k], arrive_sem.at[k], 0, outer, side))
            for side in (0, 1)
        ]

    def each(copies, method):
        for condition, copy in copies:
            pl.when(condition)(getattr(copy, method))

    def got(which, side, k, depth):
        lo, n = chunk(k)
        await_bytes(rows_of(field.at[which], lo, n, TOP, depth), halo_recv.at[which, side, k])

    @pl.when(g == 1)
    def _():
        for k in range(n_windows):
            lo, n = chunk(k)
            await_bytes(rows_of(spare, lo, n, TOP, ROWS), load_sem.at[1, k])
            each(back(k), "start")

    for k in range(n_windows):
        lo, n = chunk(k)
        await_bytes(rows_of(field.at[B], lo, n, TOP, ROWS), load_sem.at[0, k])

        @pl.when(has_far)
        def _(k=k):
            each(outside(B, k, OWN), "start")
            each(inner(B, k, OWN), "start")

        @pl.when(has_next & even)
        def _(k=k):
            shift(k).start()
            each(onward(k, SHALLOW), "start")

        @pl.when(has_next & ~even)
        def _(k=k):
            shift(k).start()
            each(onward(k, DEEP), "start")

    def arrived(k):
        lo, n = chunk(k)

        @pl.when(even)
        def _():
            await_bytes(rows_of(field.at[A], lo, n, TOP, ROWS + DEEP), arrive_sem.at[k])
            each(inner(A, k, DEEP), "start")

        @pl.when(~even)
        def _():
            await_bytes(rows_of(field.at[A], lo, n, TOP, ROWS + SHALLOW), arrive_sem.at[k])
            each(inner(A, k, SHALLOW), "start")

    def wrap(ref, lo, to, n):
        for i in range(n):
            ref[to + i] = ref[lo + i]

    def fine(src, dst, base, wide, row, rows):
        def one(i, _):
            dst[base + i, :, pl.ds(row, rows), :] = update(src, base, i, wide + 2, row, rows, FINE)
            return 0

        lax.fori_loop(1, wide + 2, one, 0, unroll=True)

    def excess(w, out, base, wide, row, rows, rough):
        def one(i, _):
            t = update(w.at[6], base, i, wide + 2, row, rows, FINE)
            if rough:
                t = t - update(w.at[STEPS - 1], base, i, wide + 2, row, rows, COARSE)
            out[base + i, :, pl.ds(row, rows), :] = t
            return 0

        lax.fori_loop(1, wide + 2, one, 0, unroll=True)

    def mend(ref, row, rows):
        lane = lax.broadcasted_iota(jnp.int32, (2, rows, LANES), 2)
        here = pl.ds(row, rows)
        ref[1, :, here, :] = jnp.where(lane < LANES // 2, ref[cols + 1, :, here, :], ref[1, :, here, :])

    def march_own(k):
        for q in range(cols // BROAD):
            @pl.when(k == q)
            def _(q=q):
                for p in range(q * BROAD // WIDE, (q + 1) * BROAD // WIDE):
                    got(B, 0, p, OWN)
                    got(B, 1, p, OWN)
                if q == cols // BROAD - 1:
                    wrap(field.at[B], 0, cols, 2)

        w = steps.at[B]
        base = BROAD * k
        fine(field.at[B], w.at[0], base, BROAD, TOP - 8, 48)
        for n in range(1, 7):
            row, rows = (TOP - 8, 48) if n < 3 else (TOP - 4, 40)
            fine(w.at[n - 1], w.at[n], base, BROAD, row, rows)
        excess(w, tau.at[B], base, BROAD, TOP, ROWS, True)

    def put(f):
        there = pl.ds(pl.multiple_of((f - 1) * LANES, LANES), LANES)
        relaxed[f, :, strip, :] = steps[A, STEPS - 1, f, :, strip, :]
        pltpu.make_async_copy(relaxed.at[f, :, strip, :], relaxed_ref.at[:, :, there], out_sem.at[0]).start()

        @pl.when(g == 0)
        def _():
            pltpu.make_async_copy(relaxed.at[f, :, strip, :], corrected_ref.at[:, :, there], out_sem.at[1]).start()

    def march_prior(k):
        for q in range(n_windows):
            @pl.when(k == q)
            def _(q=q):
                @pl.when(even)
                def _():
                    got(A, 0, q, DEEP)

                @pl.when(~even)
                def _():
                    got(A, 0, q, SHALLOW)

                if q == n_windows - 1:
                    wrap(field.at[A], 0, cols, 2)

        base = WIDE * k
        w = steps.at[A]
        row, rows = TOP - 4, 40
        fine(field.at[A], w.at[0], base, WIDE, TOP - 8, 48)
        for n in range(1, STEPS):
            fine(w.at[n - 1], w.at[n], base, WIDE, TOP - 8, 48)

        def one(f, _):
            put(f)
            return 0

        lax.fori_loop(jnp.maximum(base + 1, 2), base + WIDE + 1, one, 0)

        @pl.when(k == n_windows - 1)
        def _():
            mend(steps.at[A, STEPS - 1], TOP, ROWS)
            put(1)

        @pl.when(even)
        def _():
            for n in range(STEPS, 7):
                fine(w.at[n - 1], w.at[n], base, WIDE, row, rows)

            @pl.when(g == 0)
            def _():
                excess(w, tau.at[A], base, WIDE, row, rows, False)

            @pl.when(g > 0)
            def _():
                excess(w, tau.at[A], base, WIDE, row, rows, True)

    def put_out(ref, p, offset):
        c = lax.rem(p + offset, cols)
        pltpu.make_async_copy(
            ref.at[p, :, strip, :],
            corrected_ref.at[:, :, pl.ds(pl.multiple_of(c * LANES, LANES), LANES)],
            out_sem.at[1],
        ).start()

    def group_in(j, extra):
        await_bytes(rows_of(state, GROUP * j, GROUP, TOP - extra, ROWS + 2 * extra), chain_recv.at[j])

    def group_out(j):
        def copy(row_from, n, row_to, device):
            return pltpu.make_async_remote_copy(
                src_ref=rows_of(nxt, GROUP * j, GROUP, row_from, n),
                dst_ref=rows_of(state, GROUP * j, GROUP, row_to, n),
                send_sem=chain_send.at[j], recv_sem=chain_recv.at[j],
                device_id=(g + 2, device), device_id_type=MESH,
            )

        copy(TOP, EDGE, TOP + ROWS, down).start()
        copy(TOP + ROWS - EDGE, EDGE, TOP - EDGE, up).start()
        copy(TOP, ROWS, TOP, r).start()

    def pass_on(j, src, first):
        return pltpu.make_async_remote_copy(
            src_ref=rows_of(src, first, GROUP, TOP, ROWS),
            dst_ref=rows_of(state, GROUP * j, GROUP, TOP, ROWS),
            send_sem=pass_send.at[j], recv_sem=chain_recv.at[j],
            device_id=(g + 1, r), device_id_type=MESH,
        )

    def chain(j, _):
        base = GROUP * j
        row, rows = TOP - 4, 40

        def onward_state(src, first):
            def rough(i, _):
                nxt[base + i, :, strip, :] = update(src, first, i + 1, GROUP + 2, TOP, ROWS, COARSE) + tau[B, base + x + 2 + i, :, strip, :]
                return 0

            lax.fori_loop(0, GROUP, rough, 0, unroll=True)
            group_out(j)

        @pl.when(x > 0)
        def _():
            @pl.when(j == 0)
            def _():
                group_in(0, EDGE)
                wrap(state, 0, cols, 2)
                for i in range(GROUP):
                    put_out(state, i, x)

            @pl.when(j < n_groups - 1)
            def _():
                group_in(j + 1, EDGE)
                for i in range(GROUP):
                    put_out(state, GROUP * (j + 1) + i, x)

            def rough(i, _):
                mid[i, :, pl.ds(row, rows), :] = update(state, base, i, GROUP + 2, row, rows, COARSE) + tau[A, base + x + 1 + i, :, pl.ds(row, rows), :]
                return 0

            @pl.when(has_far)
            def _():
                lax.fori_loop(0, GROUP + 2, rough, 0, unroll=True)

            @pl.when(~has_far)
            def _():
                lax.fori_loop(1, GROUP + 1, rough, 0, unroll=True)

            @pl.when(has_far)
            def _():
                onward_state(mid, 0)

            for i in range(GROUP):
                odd_state[base + i, :, strip, :] = mid[1 + i, :, strip, :]
            pass_on(j, odd_state, base).start()

        @pl.when(x == 0)
        def _():
            onward_state(tau.at[A], base + 1)
            pass_on(j, tau.at[A], base + 2).start()

        return 0

    ahead = WIDE // GROUP
    lead = jnp.where(x == 0, 0, 1)
    per = BROAD // WIDE

    def rounds(k, _):
        now = (k >= 0) & (k < n_windows)
        for q in range(n_windows):
            @pl.when((k == q) & ((x == 0) | (q == 0)))
            def _(q=q):
                arrived(q)

        @pl.when(has_far & (k + lead < n_windows) & (lax.rem(k + lead, per) == 0))
        def _():
            march_own((k + lead) // per)

        @pl.when(now)
        def _():
            march_prior(k)

        for q in range(n_windows - 1):
            @pl.when((x > 0) & (k == q))
            def _(q=q):
                arrived(q + 1)

        @pl.when(has_far & (k == n_windows))
        def _():
            mend(tau.at[B], TOP, ROWS)
            tau[B, cols + 1] = tau[B, 1]
            for i in range(1, 5):
                tau[B, cols + 1 + i] = tau[B, 1 + i]

        @pl.when(even & (k == n_windows))
        def _():
            mend(tau.at[A], TOP - 4, 40)
            for i in range(5):
                tau[A, cols + 1 + i] = tau[A, 1 + i]

        @pl.when(even)
        def _():
            lag = jnp.maximum(x - 1, 0)
            first = jnp.maximum(ahead * (k - 1) + 1 - lag, 0)
            stop = jnp.maximum(ahead * k + 1 - lag, 0)
            lax.fori_loop(first, jnp.where(k == n_windows, n_groups, stop), chain, 0)

        return 0

    lax.fori_loop(-lead, n_windows + 1, rounds, 0)

    @pl.when(~even)
    def _():
        def one(j, _):
            group_in(j, 0)
            for i in range(GROUP):
                put_out(state, GROUP * j + i, x + 1)
            return 0

        lax.fori_loop(0, n_groups, one, 0)

    for k in range(n_windows):
        @pl.when(has_far)
        def _(k=k):
            each(outside(B, k, OWN), "wait_send")
            each(inner(B, k, OWN), "wait_send")

        @pl.when(has_next & even)
        def _(k=k):
            each(onward(k, SHALLOW), "wait_send")

        @pl.when(has_next & ~even)
        def _(k=k):
            each(onward(k, DEEP), "wait_send")

        @pl.when(has_next)
        def _(k=k):
            shift(k).wait_send()

        @pl.when(even)
        def _(k=k):
            each(inner(A, k, DEEP), "wait_send")

        @pl.when(~even)
        def _(k=k):
            each(inner(A, k, SHALLOW), "wait_send")

        @pl.when(g == 1)
        def _(k=k):
            each(back(k), "wait_send")

    @pl.when(even)
    def _():
        def one(j, _):
            pass_on(j, odd_state, 0).wait_send()

            @pl.when(has_far)
            def _():
                await_bytes(rows_of(nxt, GROUP * j, GROUP, TOP, ROWS + 2 * EDGE), chain_send.at[j])

            return 0

        lax.fori_loop(0, n_groups, one, 0)

    for i in range(2):
        await_bytes(rows_of(relaxed, 1, cols, TOP, ROWS), out_sem.at[i])


def shards(start_state, guess):
    guess = guess[0]
    width = guess.shape[2]
    cols = width // LANES
    strips = lax.axis_size("rows")
    groups = lax.axis_size("tm")
    out = jax.ShapeDtypeStruct(guess.shape, guess.dtype)
    n_windows = cols // WIDE
    n_groups = cols // GROUP

    def frames(*lead):
        return pltpu.VMEM((*lead, 2, FRAME, LANES), jnp.float32)

    dma = pltpu.SemaphoreType.DMA
    corrected, relaxed = pl.pallas_call(
        functools.partial(kernel, cols, groups, strips),
        out_shape=(out, out),
        in_specs=[pl.BlockSpec(memory_space=pltpu.HBM)] * 2,
        out_specs=(pl.BlockSpec(memory_space=pl.ANY),) * 2,
        scratch_shapes=[
            frames(2, cols + 2), frames(cols), frames(2, cols + 6), frames(2, 7, cols + 2),
            frames(cols + 1), frames(cols + 2), frames(GROUP + 2), frames(cols), frames(cols),
            dma((2, n_windows)), dma((n_windows,)), dma((n_windows,)), dma((2 * n_windows,)),
            dma((2, 2, n_windows)), dma((2, 2, n_windows)),
            dma((n_groups,)), dma((n_groups,)), dma((n_groups,)), dma((2,)),
        ],
        compiler_params=pltpu.CompilerParams(
            collective_id=0, has_side_effects=True, vmem_limit_bytes=51 * 2**20
        ),
    )(start_state, guess)
    return corrected[None], relaxed[None]


def solution(mesh):
    return jax.shard_map(
        shards,
        mesh=mesh,
        in_specs=(P(None, "rows", None), P("tm", None, "rows", None)),
        out_specs=(P("tm", None, "rows", None), P("tm", None, "rows", None)),
        check_vma=False,
    )
```
